512 devices in a mesh: year: 8 (over z), tile: 64 (over y, x, core).
Axes of the slice: x: 4, y: 8, z: 8, core: 2. Of those that a mesh axis runs over, the one named last changes fastest.
Arguments:
- eta: float32 [32, 1024, 1024], P('year', 'tile'), may hold values from -3 to 3
- counts: int32 [32, 1024, 1024], P('year', 'tile'), may hold values from 0 to 11
- mask: int32 [1024, 1024], P('tile'), may hold values 0 or 1
- kappa2: float32 [1024, 1024], P('tile'), may hold values from 0.02 to 0.3
- rho: float32 [1], replicated, may hold values from 0.5 to 0.9
Outputs:
- step: float32 [32, 1024, 1024], P('year', 'tile')
- residual: float32 [32, 1024, 1024], P('year', 'tile')
The draws below stay inside these ranges and needn't reach their ends.
All inputs are finite; a program needn't handle non-finite values. No bound on the sum of `mask` on one device may be relied on, other than what follows from the above.
Results may differ from the reference program's by a relative error of at most 0.012.
Values sent between devices are 32-bit elements; how exact they have to be, the bound alone decides.
A program may use at most 64 MiB of HBM per device.

```python
import math
import jax
import jax.numpy as jnp

NY = 1024
ITERS = 3
YEARS = 32
NX = 1024


def touch_ends(drawn, own_key, smallest, largest):
    spot = [jax.random.randint(jax.random.fold_in(own_key, axis), (), 0, length) for axis, length in enumerate(drawn.shape)]
    main_axis = drawn.shape.index(max(drawn.shape))
    neighbour = spot[:main_axis] + [(spot[main_axis] + 1) % drawn.shape[main_axis]] + spot[main_axis + 1:]
    return drawn.at[tuple(spot)].set(smallest).at[tuple(neighbour)].set(largest)


def block_levels(key, shape, pieces, least, largest):
    def one(axis_at, parts):
        draws = jax.random.uniform(jax.random.fold_in(jax.random.fold_in(key, 6), axis_at), (parts,), jnp.float32, least / len(pieces), largest / len(pieces))
        return jnp.repeat(jnp.exp(draws), shape[axis_at] // parts).reshape((-1,) + (1,) * (len(shape) - axis_at - 1))

    loudness = one(*pieces[0])
    for cut in pieces[1:]:
        loudness = loudness * one(*cut)
    return loudness


def gaussian(rng, shape, scale, reach, cuts=(), kind=jnp.bfloat16):
    factor_of = block_levels(rng, shape, cuts, -0.22, 0.18) if cuts else 1.0
    drawn = jax.random.normal(rng, shape, jnp.float32) * scale * factor_of
    return jnp.minimum(jnp.maximum(drawn, -reach), reach).astype(kind)


def setup_inputs(seed: int = 0) -> dict:
    arg_keys = jax.random.split(jax.random.key(seed), 6)
    eta = gaussian(arg_keys[0], (YEARS, NX, NY), 0.5, 3.0, ((0, 8), (1, 64)), jnp.float32)
    counts = touch_ends(jax.random.randint(arg_keys[1], (YEARS, NX, NY), 0, 12), jax.random.fold_in(arg_keys[1], 1), 0, 11).astype(jnp.int32)
    mask = touch_ends((jax.random.randint(arg_keys[2], (NX, NY), 0, 5) < 4).astype(jnp.int32), jax.random.fold_in(arg_keys[2], 1), 0, 1)
    kappa2 = jnp.clip(jnp.exp(math.log(0.3) - 2.7080503 * jax.random.uniform(arg_keys[3], (NX, NY), jnp.float32) ** block_levels(arg_keys[3], (NX, NY), ((0, 64),), -0.2, 0.2)), 0.02, 0.3)
    rho = jnp.clip(jax.random.uniform(arg_keys[4], (1,), jnp.float32, 0.5, 0.9), 0.5, 0.9)
    return dict(eta=eta, counts=counts, mask=mask, kappa2=kappa2, rho=rho)


TAU = 0.05


def kernel_apply(field, kappa2):
    padded = jnp.pad(field, ((0, 0), (1, 1), (1, 1)))
    beside_all = padded[:, 2:, 1:-1] + padded[:, :-2, 1:-1] + padded[:, 1:-1, 2:] + padded[:, 1:-1, :-2]
    return (kappa2 + 4.0) * field - beside_all


def precision_apply(field, kappa2, rho_value, hessian):
    spatial = kernel_apply(kernel_apply(field, kappa2), kappa2)
    count_years = spatial.shape[0]
    years_index = jnp.arange(count_years)
    interior = ((years_index > 0) & (years_index < count_years - 1)).astype(field.dtype)
    coupling = 1.0 + rho_value * rho_value * interior
    padded = jnp.pad(spatial, ((1, 1), (0, 0), (0, 0)))
    temporal = coupling[:, None, None] * spatial - rho_value * (padded[2:] + padded[:-2])
    return TAU * temporal + hessian * field


def reference(eta, counts, mask, kappa2, rho):
    rho_value = rho[0]
    rate = jnp.exp(eta)
    sea = mask.astype(eta.dtype)[None]
    hessian = sea * rate
    right_side = sea * (counts.astype(eta.dtype) - rate) - precision_apply(eta, kappa2, rho_value, hessian)
    step = jnp.zeros_like(eta)
    residual = right_side
    direction = right_side
    norm_now = jnp.sum(residual * residual)
    for turn in range(ITERS):
        image = precision_apply(direction, kappa2, rho_value, hessian)
        alpha = norm_now / jnp.sum(direction * image)
        step = step + alpha * direction
        residual = residual - alpha * image
        norm_next = jnp.sum(residual * residual)
        direction = residual + (norm_next / norm_now) * direction
        norm_now = norm_next
    return step, residual
```

```python
import functools
import itertools

import jax
import jax.numpy as jnp
from jax import lax
from jax.experimental import pallas as pl
from jax.experimental.pallas import tpu as pltpu
from jax.sharding import PartitionSpec as P

TAU = 0.05
SHIFTS = (1.0, 6.0, 1.0)
MESH = pl.DeviceIdType.MESH
CHIPS_X, CORES = 4, 2
YEARS, ROWS, EDGE = 4, 16, 8
TALL = ROWS + 2 * EDGE


def around(distance, size):
    return min(distance, size - distance)


def partners(sizes, pick):
    spans = [range(n) if name in pick else range(1) for name, n in sizes.items()]
    found = [g for g in itertools.product(*spans) if any(g)]
    far = lambda g: sum(around(d, n) for d, n in zip(g, sizes.values()))
    return sorted(found, key=lambda g: -far(g))


def kernel(
    slabs, strips, stages,
    eta_in, counts_in, mask_in, kappa_in, rho_in, step_out, residual_out,
    eta, counts, mask, kappa, k4, hess, b, v1, v2, v3, ys, ws, parts, got1, got2, outs,
    load_sem, send_sem, recv_sem, sum_send, sum_recv, store_sem,
):
    z, t = lax.axis_index("year"), lax.axis_index("tile")
    chips_y = strips // (CHIPS_X * CORES)
    lanes = eta.shape[-1] // 128

    def beside(dz, dt):
        return (lax.rem(z + dz + slabs, slabs), lax.rem(t + dt + strips, strips))

    def partner(g):
        dz, dy, dx, dc = g
        y, x, c = t // (CHIPS_X * CORES), lax.rem(t // CORES, CHIPS_X), lax.rem(t, CORES)
        y, x, c = lax.rem(y + dy, chips_y), lax.rem(x + dx, CHIPS_X), lax.rem(c + dc, CORES)
        return (lax.rem(z + dz, slabs), (y * CHIPS_X + x) * CORES + c)

    loads = [
        pltpu.make_async_copy(source, target, load_sem.at[i])
        for i, (source, target) in enumerate(
            [
                (eta_in, eta.at[pl.ds(2, YEARS), pl.ds(EDGE, ROWS)]),
                (kappa_in, kappa.at[pl.ds(EDGE, ROWS)]),
                (mask_in, mask.at[pl.ds(EDGE, ROWS)]),
                (counts_in, counts),
            ]
        )
    ]
    for copy in loads:
        copy.start()

    barrier = pltpu.get_barrier_semaphore()
    near = [(dz, dt) for dz in (-1, 0, 1) for dt in (-1, 0, 1) if (dz, dt) != (0, 0)]
    greeted = [partner(g) for stage in stages for g in stage] + [beside(*n) for n in near]
    for device in greeted:
        pl.semaphore_signal(barrier, inc=1, device_id=device, device_id_type=MESH)

    zero = jnp.zeros((8, 128), jnp.float32)
    for j in range(lanes):
        for ref in (ys, ws):
            ref[j, 0:8, :] = zero
            ref[j, 8 + TALL : 16 + TALL, :] = zero
    rho = rho_in[0]
    top = jnp.where(t > 0, 1.0, 0.0).astype(jnp.float32)
    bottom = jnp.where(t < strips - 1, 1.0, 0.0).astype(jnp.float32)
    inside = (top, None, None, bottom)

    sent = []

    def remote(source, target, place):
        i = len(sent)
        copy = pltpu.make_async_remote_copy(
            src_ref=source,
            dst_ref=target,
            send_sem=send_sem.at[i],
            recv_sem=recv_sem.at[i],
            device_id=beside(*place),
            device_id_type=MESH,
        )
        copy.start()
        sent.append(copy)
        return copy

    first, last = pl.ds(EDGE, EDGE), pl.ds(ROWS, EDGE)
    above, below = pl.ds(0, EDGE), pl.ds(EDGE + ROWS, EDGE)
    whole = pl.ds(EDGE, ROWS)

    def send_year(field, lead, year, up, down):
        copies = []
        for dz, here, there in ((1, *up), (-1, *down)):
            copies.append(remote(field.at[here, last], field.at[there, above], (dz, 1)))
            copies.append(remote(field.at[here, first], field.at[there, below], (dz, -1)))
        for dz, here, there in ((1, *up), (-1, *down)):
            copies.append(remote(field.at[here, whole], field.at[there, whole], (dz, 0)))
        return copies

    def send_strip(field):
        return [
            remote(field.at[..., last, :], field.at[..., above, :], (0, 1)),
            remote(field.at[..., first, :], field.at[..., below, :], (0, -1)),
        ]

    def beside_sum(ref, r):
        lane = lax.broadcasted_iota(jnp.int32, (8, 128), 1)
        at = 8 + 8 * r
        core = [ref[j, at : at + 8, :] for j in range(lanes)]
        right = [pltpu.roll(core[j], 1, 1) for j in range(lanes)]
        left = [pltpu.roll(core[j], 127, 1) for j in range(lanes)]
        sums = []
        for j in range(lanes):
            west = jnp.where(lane == 0, right[j - 1] if j else 0.0, right[j])
            east = jnp.where(lane == 127, left[j + 1] if j + 1 < lanes else 0.0, left[j])
            north, south = ref[j, at - 1 : at + 7, :], ref[j, at + 1 : at + 9, :]
            sums.append((north + south) + (west + east))
        return core, sums

    def tile_of(ref, i, r, j):
        return ref[i, 8 * r : 8 * r + 8, 128 * j : 128 * j + 128]

    def precision(field, i, year, tiles, finish):
        g = z * YEARS + year
        final = slabs * YEARS - 1
        c = TAU * jnp.where((g > 0) & (g < final), 1.0 + rho * rho, 1.0)
        before = TAU * jnp.where(g > 0, rho, 0.0)
        after = TAU * jnp.where(g < final, rho, 0.0)
        for r in range(4):
            f = inside[r]
            cr, br, ar = (c, before, after) if f is None else (c * f, before * f, after * f)
            for j in range(lanes):
                value = cr * tile_of(field, i, r, j)
                value -= br * tile_of(field, i - 1, r, j) + ar * tile_of(field, i + 1, r, j)
                ys[j, 8 + 8 * r : 16 + 8 * r, :] = value
        for r in range(4):
            core, sums = beside_sum(ys, r)
            for j in range(lanes):
                value = tile_of(k4, 0, r, j) * core[j] - sums[j]
                if inside[r] is not None:
                    value *= inside[r]
                ws[j, 8 + 8 * r : 16 + 8 * r, :] = value
        for r in tiles:
            core, sums = beside_sum(ws, r)
            for j in range(lanes):
                finish(r, j, tile_of(k4, 0, r, j) * core[j] - sums[j])

    for copy in loads[:3]:
        copy.wait()
    pl.semaphore_wait(barrier, len(greeted))
    eta_near = send_year(eta, 2, 1, (5, 1), (2, 6))
    eta_strip = send_strip(eta.at[pl.ds(2, YEARS)])
    kappa_strip = send_strip(kappa)
    mask_strip = send_strip(mask)
    eta_far = send_year(eta, 2, 2, (4, 0), (3, 7))
    loads[3].wait()

    for copy in kappa_strip:
        copy.wait_recv()
    for r in range(4):
        k4[0, 8 * r : 8 * r + 8, :] = kappa[8 * r : 8 * r + 8, :] + 4.0
    for copy in eta_near + eta_strip:
        copy.wait_recv()

    def right_side(year):
        def finish(r, j, value):
            x = tile_of(eta, year + 2, r, j)
            rate = jnp.exp(x)
            sea = mask[8 * r : 8 * r + 8, 128 * j : 128 * j + 128].astype(jnp.float32)
            caught = counts[year, 8 * r - 8 : 8 * r, 128 * j : 128 * j + 128].astype(jnp.float32)
            b[year + 3, 8 * r : 8 * r + 8, 128 * j : 128 * j + 128] = sea * (caught - rate) - (
                value + sea * rate * x
            )

        precision(eta, year + 2, year, (1, 2), finish)

    @pl.loop(0, 2)
    def _(k):
        right_side(3 * k)

    b_near = send_year(b, 3, 1, (6, 2), (3, 7))

    @pl.loop(1, 3)
    def _(k):
        right_side(k)

    b_strip = send_strip(b.at[pl.ds(3, YEARS)])
    b_next = send_year(b, 3, 2, (5, 1), (4, 8))
    b_far = send_year(b, 3, 3, (4, 0), (5, 9))

    for copy in mask_strip + eta_far:
        copy.wait_recv()

    @pl.loop(0, YEARS + 4)
    def _(k):
        for r in range(4):
            for j in range(lanes):
                at = (slice(8 * r, 8 * r + 8), slice(128 * j, 128 * j + 128))
                sea = mask[at].astype(jnp.float32)
                hess[(k, *at)] = sea * jnp.exp(eta[(k, *at)])

    def power(field, lead, into, into_lead, shift, year, terms=None):
        found = []

        def finish(r, j, value):
            x = tile_of(field, year + lead, r, j)
            new = value + (tile_of(hess, year + 2, r, j) - shift) * x
            if into is v3:
                into[year, 8 * r - 8 : 8 * r, 128 * j : 128 * j + 128] = new
            else:
                into[year + into_lead, 8 * r : 8 * r + 8, 128 * j : 128 * j + 128] = new
            if terms is not None and r in (1, 2):
                found.append(terms(x, new, lambda ref, lead: tile_of(ref, year + lead, r, j)))

        precision(field, year + lead, year, (1, 2) if into is v3 else range(4), finish)
        if terms is None:
            return None
        while len(found) > 1:
            found = [tuple(map(jnp.add, p, q)) for p, q in zip(found[::2], found[1::2])]
        return found[0]

    def own(field, lead, into, into_lead, shift, terms, count):
        def body(year, sums):
            found = power(field, lead, into, into_lead, shift, year, terms)
            return tuple(map(jnp.add, sums, found))

        return lax.fori_loop(0, YEARS, body, (zero,) * count)

    for copy in b_near + b_strip:
        copy.wait_recv()
    moments = own(b, 3, v1, 2, SHIFTS[0], lambda x, n, at: (x * x, x * n, n * n), 3)
    for copy in b_next:
        copy.wait_recv()

    @pl.loop(0, 2)
    def _(k):
        power(b, 3, v1, 2, SHIFTS[0], 5 * k - 1)

    moments += own(v1, 2, v2, 1, SHIFTS[1], lambda x, n, at: (at(b, 3) * n, x * n, n * n), 3)
    for copy in b_far:
        copy.wait_recv()

    @pl.loop(0, 2)
    def _(k):
        power(b, 3, v1, 2, SHIFTS[0], 7 * k - 2)

    @pl.loop(0, 2)
    def _(k):
        power(v1, 2, v2, 1, SHIFTS[1], 5 * k - 1)

    moments += own(v2, 1, v3, 0, SHIFTS[2], lambda x, n, at: (at(v1, 2) * n, x * n), 2)

    row = lax.broadcasted_iota(jnp.int32, (8, 128), 0)
    mine = zero
    for k, value in enumerate(moments):
        mine = jnp.where(row == k, jnp.sum(value, axis=0, keepdims=True), mine)
    for s, (stage, got) in enumerate(zip(stages, (got1, got2))):
        parts[s] = mine
        for i, g in enumerate(stage):
            pltpu.make_async_remote_copy(
                src_ref=parts.at[s],
                dst_ref=got.at[i],
                send_sem=sum_send.at[s],
                recv_sem=sum_recv.at[s],
                device_id=partner(g),
                device_id_type=MESH,
            ).start()
        pltpu.make_async_copy(got, got, sum_recv.at[s]).wait()
        mine += jnp.sum(got[...], axis=0)
    total = jnp.broadcast_to(jnp.sum(mine, axis=1, keepdims=True), (8, 128))
    m00, m01, m11, m02, m12, m22, m13, m23 = [total[k : k + 1, :] for k in range(8)]
    gram = [[m00, m01, m02, m12], [m01, m11, m12, m13], [m02, m12, m22, m23]]

    def product(p, q):
        terms = [a * c * gram[i][j] for i, a in enumerate(p) for j, c in enumerate(q)]
        return functools.reduce(jnp.add, terms)

    def times_q(p):
        return [
            (SHIFTS[i] * p[i] if i < len(p) else 0.0) + (p[i - 1] if i else 0.0)
            for i in range(len(p) + 1)
        ]

    def plus(p, q, scale):
        size = max(len(p), len(q))
        p, q = list(p) + [0.0] * (size - len(p)), list(q) + [0.0] * (size - len(q))
        return [a + scale * c for a, c in zip(p, q)]

    one = jnp.ones((1, 128), jnp.float32)
    step, residual, direction, norm_now = [0.0 * one], [one], [one], m00
    for turn in range(3):
        image = times_q(direction)
        alpha = norm_now / product(direction, image)
        step = plus(step, direction, alpha)
        residual = plus(residual, image, -alpha)
        if turn < 2:
            norm_next = product(residual, residual)
            direction = plus(residual, direction, norm_next / norm_now)
            norm_now = norm_next

    def write(year):
        return [
            pltpu.make_async_copy(outs.at[i, year], out.at[year], store_sem.at[i, year])
            for i, out in enumerate((step_out, residual_out))
        ]

    for year in range(YEARS):
        for r in (1, 2):
            for j in range(lanes):
                at = (slice(8 * r - 8, 8 * r), slice(128 * j, 128 * j + 128))
                basis = [
                    tile_of(b, year + 3, r, j),
                    tile_of(v1, year + 2, r, j),
                    tile_of(v2, year + 1, r, j),
                    v3[(year, *at)],
                ]
                for i, weights in enumerate((step, residual)):
                    outs[(i, year, *at)] = functools.reduce(
                        jnp.add, [w * v for w, v in zip(weights, basis)]
                    )
        for copy in write(year):
            copy.start()
    for year in range(YEARS):
        for copy in write(year):
            copy.wait()
    for copy in sent:
        copy.wait_send()
    for s, got in enumerate((got1, got2)):
        pltpu.make_async_copy(got, got, sum_send.at[s]).wait()


def solution(mesh):
    slabs, strips = mesh.shape["year"], mesh.shape["tile"]
    sizes = {"z": slabs, "y": strips // (CHIPS_X * CORES), "x": CHIPS_X, "core": CORES}
    stages = [partners(sizes, ("z", "x")), partners(sizes, ("y", "core"))]

    def on_device(eta, counts, mask, kappa2, rho):
        width = eta.shape[-1]
        f32 = jnp.float32
        field = lambda years: pltpu.VMEM((years, TALL, width), f32)
        out = jax.ShapeDtypeStruct(eta.shape, f32)
        return pl.pallas_call(
            functools.partial(kernel, slabs, strips, stages),
            out_shape=(out, out),
            in_specs=[pl.BlockSpec(memory_space=pl.ANY)] * 4
            + [pl.BlockSpec(memory_space=pltpu.SMEM)],
            out_specs=(pl.BlockSpec(memory_space=pl.ANY),) * 2,
            scratch_shapes=[
                field(YEARS + 4),
                pltpu.VMEM((YEARS, ROWS, width), jnp.int32),
                pltpu.VMEM((TALL, width), jnp.int32),
                pltpu.VMEM((TALL, width), f32),
                field(1),
                field(YEARS + 4),
                field(YEARS + 6),
                field(YEARS + 4),
                field(YEARS + 2),
                pltpu.VMEM((YEARS, ROWS, width), f32),
                pltpu.VMEM((width // 128, TALL + 16, 128), f32),
                pltpu.VMEM((width // 128, TALL + 16, 128), f32),
                pltpu.VMEM((2, 8, 128), f32),
                pltpu.VMEM((len(stages[0]), 8, 128), f32),
                pltpu.VMEM((len(stages[1]), 8, 128), f32),
                pltpu.VMEM((2, YEARS, ROWS, width), f32),
                pltpu.SemaphoreType.DMA((4,)),
                pltpu.SemaphoreType.DMA((40,)),
                pltpu.SemaphoreType.DMA((40,)),
                pltpu.SemaphoreType.DMA((2,)),
                pltpu.SemaphoreType.DMA((2,)),
                pltpu.SemaphoreType.DMA((2, YEARS)),
            ],
            compiler_params=pltpu.CompilerParams(
                collective_id=0, has_side_effects=True, vmem_limit_bytes=40 << 20
            ),
        )(eta, counts, mask, kappa2, rho)

    return jax.shard_map(
        on_device,
        mesh=mesh,
        in_specs=(
            P("year", "tile", None),
            P("year", "tile", None),
            P("tile", None),
            P("tile", None),
            P(),
        ),
        out_specs=(P("year", "tile", None),) * 2,
        check_vma=False,
    )
```

```python
import functools
import itertools

import jax
import jax.numpy as jnp
from jax import lax
from jax.experimental import pallas as pl
from jax.experimental.pallas import tpu as pltpu
from jax.sharding import PartitionSpec as P

TAU = 0.05
SHIFTS = (1.0, 6.0, 1.0)
MESH = pl.DeviceIdType.MESH
CHIPS_X, CORES = 4, 2
YEARS, ROWS, EDGE = 4, 16, 8
TALL = ROWS + 2 * EDGE


def around(distance, size):
    return min(distance, size - distance)


def partners(sizes, pick):
    spans = [range(n) if name in pick else range(1) for name, n in sizes.items()]
    found = [g for g in itertools.product(*spans) if any(g)]
    far = lambda g: sum(around(d, n) for d, n in zip(g, sizes.values()))
    return sorted(found, key=lambda g: -far(g))


def kernel(
    slabs, strips, stages,
    eta_in, counts_in, mask_in, kappa_in, rho_in, own0, own1, own2, v3, *rest,
):
    *weights_out, eta, counts, mask, kappa, k4, hess, b, v1, v2, ys, ws = rest[:18]
    parts, got1, got2, load_sem, send_sem, recv_sem, sum_send, sum_recv = rest[18:]
    z, t = lax.axis_index("year"), lax.axis_index("tile")
    core = lax.rem(t, CORES)
    chips_y = strips // (CHIPS_X * CORES)
    lanes = eta.shape[-1] // 128

    def beside(dz, dt):
        return (lax.rem(z + dz + slabs, slabs), lax.rem(t + dt + strips, strips))

    def partner(g):
        dz, dy, dx, dc = g
        y, x, c = t // (CHIPS_X * CORES), lax.rem(t // CORES, CHIPS_X), lax.rem(t, CORES)
        y, x, c = lax.rem(y + dy, chips_y), lax.rem(x + dx, CHIPS_X), lax.rem(c + dc, CORES)
        return (lax.rem(z + dz, slabs), (y * CHIPS_X + x) * CORES + c)

    loads = [
        pltpu.make_async_copy(source, target, load_sem.at[i])
        for i, (source, target) in enumerate(
            [
                (eta_in, eta.at[pl.ds(2, YEARS), pl.ds(EDGE, ROWS)]),
                (kappa_in, kappa.at[0, pl.ds(EDGE, ROWS)]),
                (mask_in, mask.at[0, pl.ds(EDGE, ROWS)]),
                (counts_in, counts),
            ]
        )
    ]
    for copy in loads:
        copy.start()

    barrier = pltpu.get_barrier_semaphore()
    near = [(dz, dt) for dz in (-1, 0, 1) for dt in (-1, 0, 1) if (dz, dt) != (0, 0)]
    greeted = [partner(g) for stage in stages for g in stage] + [beside(*n) for n in near]
    for device in greeted:
        pl.semaphore_signal(barrier, inc=1, device_id=device, device_id_type=MESH)

    zero = jnp.zeros((8, 128), jnp.float32)
    for j in range(lanes):
        for ref in (ys, ws):
            ref[j, 0:8, :] = zero
            ref[j, 8 + TALL : 16 + TALL, :] = zero
    rho = rho_in[0]
    top = jnp.where(t > 0, 1.0, 0.0).astype(jnp.float32)
    bottom = jnp.where(t < strips - 1, 1.0, 0.0).astype(jnp.float32)
    inside = (top, None, None, bottom)

    sent = []

    def remote(*options):
        i = len(sent)
        copies = [
            pltpu.make_async_remote_copy(
                src_ref=source,
                dst_ref=target,
                send_sem=send_sem.at[i],
                recv_sem=recv_sem.at[i],
                device_id=beside(*place),
                device_id_type=MESH,
            )
            for source, target, place in options
        ]
        if len(copies) == 1:
            copies[0].start()
        else:
            for c, copy in enumerate(copies):
                pl.when(core == c)(copy.start)
        sent.append(copies[0])
        return copies[0]

    def arrive(copies):
        for copy in copies:
            copy.wait_recv()

    whole = pl.ds(EDGE, ROWS)

    def down_strip(field, here, there, n, dz):
        source, target = pl.ds(EDGE + ROWS - n, n), pl.ds(EDGE - n, n)
        return field.at[here, source], field.at[there, target], (dz, 1)

    def up_strip(field, here, there, n, dz):
        source, target = pl.ds(EDGE, n), pl.ds(EDGE + ROWS, n)
        return field.at[here, source], field.at[there, target], (dz, -1)

    def send_corners(field, steps, n):
        return [
            remote(strip(field, here, there, n, dz))
            for dz, here, there in steps
            for strip in (down_strip, up_strip)
        ]

    def send_outer(field, steps, n):
        return [
            remote(up_strip(field, here, there, n, dz), down_strip(field, here, there, n, dz))
            for dz, here, there in steps
        ]

    def share_inner(field, steps, n):
        return [
            remote(down_strip(field, there, there, n, 0), up_strip(field, there, there, n, 0))
            for _, _, there in steps
        ]

    def send_whole(field, steps):
        return [
            remote((field.at[here, whole], field.at[there, whole], (dz, 0)))
            for dz, here, there in steps
        ]

    def send_strips(field, years, n):
        return [remote(strip(field, years, years, n, 0)) for strip in (down_strip, up_strip)]

    def beside_sum(ref, r):
        lane = lax.broadcasted_iota(jnp.int32, (8, 128), 1)
        at = 8 + 8 * r
        core = [ref[j, at : at + 8, :] for j in range(lanes)]
        right = [pltpu.roll(core[j], 1, 1) for j in range(lanes)]
        left = [pltpu.roll(core[j], 127, 1) for j in range(lanes)]
        sums = []
        for j in range(lanes):
            west = jnp.where(lane == 0, right[j - 1] if j else 0.0, right[j])
            east = jnp.where(lane == 127, left[j + 1] if j + 1 < lanes else 0.0, left[j])
            north, south = ref[j, at - 1 : at + 7, :], ref[j, at + 1 : at + 9, :]
            sums.append((north + south) + (west + east))
        return core, sums

    def tile_of(ref, i, r, j):
        return ref[i, 8 * r : 8 * r + 8, 128 * j : 128 * j + 128]

    def precision(field, i, year, tiles, finish):
        g = z * YEARS + year
        final = slabs * YEARS - 1
        c = TAU * jnp.where((g > 0) & (g < final), 1.0 + rho * rho, 1.0)
        before = TAU * jnp.where(g > 0, rho, 0.0)
        after = TAU * jnp.where(g < final, rho, 0.0)
        for r in range(4):
            f = inside[r]
            cr, br, ar = (c, before, after) if f is None else (c * f, before * f, after * f)
            for j in range(lanes):
                value = cr * tile_of(field, i, r, j)
                value -= br * tile_of(field, i - 1, r, j) + ar * tile_of(field, i + 1, r, j)
                ys[j, 8 + 8 * r : 16 + 8 * r, :] = value
        for r in range(4):
            core, sums = beside_sum(ys, r)
            for j in range(lanes):
                value = tile_of(k4, 0, r, j) * core[j] - sums[j]
                if inside[r] is not None:
                    value *= inside[r]
                ws[j, 8 + 8 * r : 16 + 8 * r, :] = value
        for r in tiles:
            core, sums = beside_sum(ws, r)
            for j in range(lanes):
                finish(r, j, tile_of(k4, 0, r, j) * core[j] - sums[j])

    for copy in loads[:3]:
        copy.wait()
    pl.semaphore_wait(barrier, len(greeted))
    eta_steps = [[(1, 6 - k, 2 - k), (-1, 1 + k, 5 + k)] for k in (1, 2)]
    eta_near = send_corners(eta, eta_steps[0], 4)
    eta_near += send_whole(eta, eta_steps[0])
    eta_near += send_strips(eta, pl.ds(2, YEARS), 4)
    kappa_strip = send_strips(kappa, 0, 8)
    mask_strip = send_strips(mask, 0, 8)
    eta_far = send_whole(eta, eta_steps[1])
    eta_far += send_corners(eta, eta_steps[1], 4)
    loads[3].wait()

    arrive(kappa_strip)
    for r in range(4):
        k4[0, 8 * r : 8 * r + 8, :] = kappa[0, 8 * r : 8 * r + 8, :] + 4.0
    arrive(eta_near)

    def right_side(year):
        def finish(r, j, value):
            x = tile_of(eta, year + 2, r, j)
            rate = jnp.exp(x)
            sea = tile_of(mask, 0, r, j).astype(jnp.float32)
            caught = counts[year, 8 * r - 8 : 8 * r, 128 * j : 128 * j + 128].astype(jnp.float32)
            new = sea * (caught - rate) - (value + sea * rate * x)
            b[year + 3, 8 * r : 8 * r + 8, 128 * j : 128 * j + 128] = new
            own0[year, 8 * r - 8 : 8 * r, 128 * j : 128 * j + 128] = new

        precision(eta, year + 2, year, (1, 2), finish)

    b_steps = [[(1, 7 - k, 3 - k), (-1, 2 + k, 6 + k)] for k in (1, 2, 3)]
    whole_b, outer_b = [None] * 3, [None] * 3

    def send_b(k):
        whole_b[k] = send_whole(b, b_steps[k])
        outer_b[k] = send_outer(b, b_steps[k], 6)

    @pl.loop(0, 2)
    def _(k):
        right_side(3 * k)

    send_b(0)

    @pl.loop(1, 3)
    def _(k):
        right_side(k)

    b_strips = send_strips(b, pl.ds(3, YEARS), 6)
    send_b(1)
    send_b(2)

    arrive(mask_strip + eta_far)

    @pl.loop(0, YEARS + 4)
    def _(k):
        for r in range(4):
            for j in range(lanes):
                at = (slice(8 * r, 8 * r + 8), slice(128 * j, 128 * j + 128))
                sea = mask[(0, *at)].astype(jnp.float32)
                hess[(k, *at)] = sea * jnp.exp(eta[(k, *at)])

    def power(field, lead, into, into_lead, shift, year, terms=None):
        found = []

        def finish(r, j, value):
            x = tile_of(field, year + lead, r, j)
            new = value + (tile_of(hess, year + 2, r, j) - shift) * x
            if into is v3:
                into[year, 8 * r - 8 : 8 * r, 128 * j : 128 * j + 128] = new
            else:
                into[year + into_lead, 8 * r : 8 * r + 8, 128 * j : 128 * j + 128] = new
            if terms is not None and r in (1, 2):
                if into is not v3:
                    keep = own1 if into is v1 else own2
                    keep[year, 8 * r - 8 : 8 * r, 128 * j : 128 * j + 128] = new
                found.append(terms(x, new, lambda ref, lead: tile_of(ref, year + lead, r, j)))

        precision(field, year + lead, year, (1, 2) if into is v3 else range(4), finish)
        if terms is None:
            return None
        while len(found) > 1:
            found = [tuple(map(jnp.add, p, q)) for p, q in zip(found[::2], found[1::2])]
        return found[0]

    first = functools.partial(power, b, 3, v1, 2, SHIFTS[0])
    second = functools.partial(power, v1, 2, v2, 1, SHIFTS[1])
    third = functools.partial(power, v2, 1, v3, 0, SHIFTS[2])

    def receive_b(k):
        arrive(whole_b[k])
        return outer_b[k] + share_inner(b, b_steps[k], 6)

    def own(step, years, terms, count):
        def body(i, sums):
            return tuple(map(jnp.add, sums, step(years(i), terms)))

        return lax.fori_loop(0, 2, body, (zero,) * count)

    edge_years, inner_years = (lambda i: 3 * i), (lambda i: 1 + i)
    terms = lambda x, n, at: (x * x, x * n, n * n)
    corners = receive_b(0)
    arrive(b_strips)
    moments = own(first, inner_years, terms, 3)
    arrive(corners)
    moments = tuple(map(jnp.add, moments, own(first, edge_years, terms, 3)))
    arrive(receive_b(1))

    @pl.loop(0, 2)
    def _(k):
        first(5 * k - 1)

    corners = receive_b(2)
    terms = lambda x, n, at: (at(b, 3) * n, x * n, n * n)
    found = own(second, inner_years, terms, 3)
    found = tuple(map(jnp.add, found, own(second, edge_years, terms, 3)))
    moments += found
    arrive(corners)

    @pl.loop(0, 2)
    def _(k):
        first(7 * k - 2)

    @pl.loop(0, 2)
    def _(k):
        second(5 * k - 1)

    terms = lambda x, n, at: (at(v1, 2) * n, x * n)
    found = own(third, inner_years, terms, 2)
    found = tuple(map(jnp.add, found, own(third, edge_years, terms, 2)))
    moments += found

    row = lax.broadcasted_iota(jnp.int32, (8, 128), 0)
    group = lax.broadcasted_iota(jnp.int32, (8, 128), 1) // 16
    mine = zero
    for k, value in enumerate(moments):
        mine = jnp.where(row == k, jnp.sum(value, axis=0, keepdims=True), mine)
    for shift in (64, 32, 16):
        mine += pltpu.roll(mine, shift, 1)
    mine = jnp.sum(jnp.where(row == group, mine, 0.0), axis=0, keepdims=True)
    for s, (stage, got) in enumerate(zip(stages, (got1, got2))):
        parts[s] = mine
        for i, g in enumerate(stage):
            pltpu.make_async_remote_copy(
                src_ref=parts.at[s],
                dst_ref=got.at[i],
                send_sem=sum_send.at[s],
                recv_sem=sum_recv.at[s],
                device_id=partner(g),
                device_id_type=MESH,
            ).start()
        pltpu.make_async_copy(got, got, sum_recv.at[s]).wait()
        mine += jnp.sum(got[...], axis=0)
    total = jnp.where(row == group, mine, 0.0)
    total = jnp.broadcast_to(jnp.sum(total, axis=1, keepdims=True), (8, 128))
    m00, m01, m11, m02, m12, m22, m13, m23 = [total[k : k + 1, :] for k in range(8)]
    gram = [[m00, m01, m02, m12], [m01, m11, m12, m13], [m02, m12, m22, m23]]

    def product(p, q):
        terms = [a * c * gram[i][j] for i, a in enumerate(p) for j, c in enumerate(q)]
        return functools.reduce(jnp.add, terms)

    def times_q(p):
        return [
            (SHIFTS[i] * p[i] if i < len(p) else 0.0) + (p[i - 1] if i else 0.0)
            for i in range(len(p) + 1)
        ]

    def plus(p, q, scale):
        size = max(len(p), len(q))
        p, q = list(p) + [0.0] * (size - len(p)), list(q) + [0.0] * (size - len(q))
        return [a + scale * c for a, c in zip(p, q)]

    one = jnp.ones((1, 128), jnp.float32)
    step, residual, direction, norm_now = [0.0 * one], [one], [one], m00
    for turn in range(3):
        image = times_q(direction)
        alpha = norm_now / product(direction, image)
        step = plus(step, direction, alpha)
        residual = plus(residual, image, -alpha)
        if turn < 2:
            norm_next = product(residual, residual)
            direction = plus(residual, direction, norm_next / norm_now)
            norm_now = norm_next

    for out, value in zip(weights_out, step + residual):
        for j in range(lanes):
            out[:, 128 * j : 128 * j + 128] = value

    for copy in sent:
        copy.wait_send()
    for s, got in enumerate((got1, got2)):
        pltpu.make_async_copy(got, got, sum_send.at[s]).wait()


def solution(mesh):
    slabs, strips = mesh.shape["year"], mesh.shape["tile"]
    sizes = {"z": slabs, "y": strips // (CHIPS_X * CORES), "x": CHIPS_X, "core": CORES}
    stages = [partners(sizes, ("z", "x")), partners(sizes, ("y", "core"))]

    def on_device(eta, counts, mask, kappa2, rho):
        width = eta.shape[-1]
        f32 = jnp.float32
        field = lambda years: pltpu.VMEM((years, TALL, width), f32)
        out = jax.ShapeDtypeStruct(eta.shape, f32)
        args = [pltpu.with_memory_space_constraint(a, pltpu.HBM) for a in (eta, counts, mask, kappa2)]
        v0, v1, v2, v3, *weights = pl.pallas_call(
            functools.partial(kernel, slabs, strips, stages),
            out_shape=(out,) * 4 + (jax.ShapeDtypeStruct((1, width), f32),) * 7,
            in_specs=[pl.BlockSpec(memory_space=pltpu.HBM)] * 4
            + [pl.BlockSpec(memory_space=pltpu.SMEM)],
            out_specs=(pl.BlockSpec(memory_space=pltpu.VMEM),) * 11,
            scratch_shapes=[
                field(YEARS + 4),
                pltpu.VMEM((YEARS, ROWS, width), jnp.int32),
                pltpu.VMEM((1, TALL, width), jnp.int32),
                field(1),
                field(1),
                field(YEARS + 4),
                field(YEARS + 6),
                field(YEARS + 4),
                field(YEARS + 2),
                pltpu.VMEM((width // 128, TALL + 16, 128), f32),
                pltpu.VMEM((width // 128, TALL + 16, 128), f32),
                pltpu.VMEM((2, 1, 128), f32),
                pltpu.VMEM((len(stages[0]), 1, 128), f32),
                pltpu.VMEM((len(stages[1]), 1, 128), f32),
                pltpu.SemaphoreType.DMA((4,)),
                pltpu.SemaphoreType.DMA((40,)),
                pltpu.SemaphoreType.DMA((40,)),
                pltpu.SemaphoreType.DMA((2,)),
                pltpu.SemaphoreType.DMA((2,)),
            ],
            compiler_params=pltpu.CompilerParams(
                collective_id=0, has_side_effects=True, vmem_limit_bytes=40 << 20
            ),
        )(*args, rho)
        of = lambda weights, basis: functools.reduce(jnp.add, map(jnp.multiply, weights, basis))
        return of(weights[:3], (v0, v1, v2)), of(weights[3:], (v0, v1, v2, v3))

    return jax.shard_map(
        on_device,
        mesh=mesh,
        in_specs=(
            P("year", "tile", None),
            P("year", "tile", None),
            P("tile", None),
            P("tile", None),
            P(),
        ),
        out_specs=(P("year", "tile", None),) * 2,
        check_vma=False,
    )
```

```python
import functools
import itertools

import jax
import jax.numpy as jnp
from jax import lax
from jax.experimental import pallas as pl
from jax.experimental.pallas import tpu as pltpu
from jax.sharding import PartitionSpec as P

TAU = 0.05
SHIFTS = (1.0, 6.0, 1.0)
MESH = pl.DeviceIdType.MESH
CHIPS_X, CORES = 4, 2
YEARS, ROWS, EDGE = 4, 16, 8
TALL = ROWS + 2 * EDGE


def around(distance, size):
    return min(distance, size - distance)


def partners(sizes, pick):
    spans = [range(n) if name in pick else range(1) for name, n in sizes.items()]
    found = [g for g in itertools.product(*spans) if any(g)]
    far = lambda g: sum(around(d, n) for d, n in zip(g, sizes.values()))
    return sorted(found, key=lambda g: -far(g))


def reach(sizes, **steps):
    found = []
    for i, (name, n) in enumerate(sizes.items()):
        for step in steps.get(name, ()):
            g = tuple(step % n if k == i else 0 for k in range(len(sizes)))
            if any(g) and g not in found:
                found.append(g)
    return found


def kernel(
    slabs, strips, stages, tokens,
    eta_in, counts_in, mask_in, kappa_in, rho_in, own0, own1, own2, v3, *rest,
):
    *weights_out, eta, counts, mask, kappa, k4, hess, b, v1, v2, ys, ws = rest[:18]
    parts, got1, got2, load_sem, send_sem, recv_sem, sum_send, sum_recv, heard = rest[18:]
    z, t = lax.axis_index("year"), lax.axis_index("tile")
    core = lax.rem(t, CORES)
    chips_y = strips // (CHIPS_X * CORES)
    lanes = eta.shape[-1] // 128

    def beside(dz, dt):
        return (lax.rem(z + dz + slabs, slabs), lax.rem(t + dt + strips, strips))

    def partner(g):
        dz, dy, dx, dc = g
        y, x, c = t // (CHIPS_X * CORES), lax.rem(t // CORES, CHIPS_X), lax.rem(t, CORES)
        y, x, c = lax.rem(y + dy, chips_y), lax.rem(x + dx, CHIPS_X), lax.rem(c + dc, CORES)
        return (lax.rem(z + dz, slabs), (y * CHIPS_X + x) * CORES + c)

    loads = [
        pltpu.make_async_copy(source, target, load_sem.at[i])
        for i, (source, target) in enumerate(
            [
                (eta_in, eta.at[pl.ds(2, YEARS), pl.ds(EDGE, ROWS)]),
                (kappa_in, kappa.at[0, pl.ds(EDGE, ROWS)]),
                (mask_in, mask.at[0, pl.ds(EDGE, ROWS)]),
                (counts_in, counts),
            ]
        )
    ]
    for copy in loads:
        copy.start()

    barrier = pltpu.get_barrier_semaphore()
    near = [(dz, dt) for dz in (-1, 0, 1) for dt in (-1, 0, 1) if (dz, dt) != (0, 0)]
    greeted = [beside(*n) for n in near] + [partner(g) for g in tokens[0] if not g[0]]
    for device in greeted:
        pl.semaphore_signal(barrier, inc=1, device_id=device, device_id_type=MESH)

    zero = jnp.zeros((8, 128), jnp.float32)
    for j in range(lanes):
        for ref in (ys, ws):
            ref[j, 0:8, :] = zero
            ref[j, 8 + TALL : 16 + TALL, :] = zero
    rho = rho_in[0]
    top = jnp.where(t > 0, 1.0, 0.0).astype(jnp.float32)
    bottom = jnp.where(t < strips - 1, 1.0, 0.0).astype(jnp.float32)
    inside = (top, None, None, bottom)

    def tell(i):
        for g in tokens[i]:
            pl.semaphore_signal(
                heard.at[i], inc=1, device_id=partner(g), device_id_type=MESH
            )

    def hear(i):
        if tokens[i]:
            pl.semaphore_wait(heard.at[i], len(tokens[i]))

    sent = []

    def remote(*options):
        i = len(sent)
        copies = [
            pltpu.make_async_remote_copy(
                src_ref=source,
                dst_ref=target,
                send_sem=send_sem.at[i],
                recv_sem=recv_sem.at[i],
                device_id=beside(*place),
                device_id_type=MESH,
            )
            for source, target, place in options
        ]
        if len(copies) == 1:
            copies[0].start()
        else:
            for c, copy in enumerate(copies):
                pl.when(core == c)(copy.start)
        sent.append(copies[0])
        return copies[0]

    def arrive(copies):
        for copy in copies:
            copy.wait_recv()

    whole = pl.ds(EDGE, ROWS)

    def down_strip(field, here, there, n, dz):
        source, target = pl.ds(EDGE + ROWS - n, n), pl.ds(EDGE - n, n)
        return field.at[here, source], field.at[there, target], (dz, 1)

    def up_strip(field, here, there, n, dz):
        source, target = pl.ds(EDGE, n), pl.ds(EDGE + ROWS, n)
        return field.at[here, source], field.at[there, target], (dz, -1)

    def send_corners(field, steps, n):
        return [
            remote(strip(field, here, there, n, dz))
            for dz, here, there in steps
            for strip in (down_strip, up_strip)
        ]

    def send_outer(field, steps, n):
        return [
            remote(up_strip(field, here, there, n, dz), down_strip(field, here, there, n, dz))
            for dz, here, there in steps
        ]

    def share_inner(field, steps, n):
        return [
            remote(down_strip(field, there, there, n, 0), up_strip(field, there, there, n, 0))
            for _, _, there in steps
        ]

    def send_whole(field, steps):
        return [
            remote((field.at[here, whole], field.at[there, whole], (dz, 0)))
            for dz, here, there in steps
        ]

    def send_strips(field, years, n):
        return [remote(strip(field, years, years, n, 0)) for strip in (down_strip, up_strip)]

    def beside_sum(ref, r):
        lane = lax.broadcasted_iota(jnp.int32, (8, 128), 1)
        at = 8 + 8 * r
        core = [ref[j, at : at + 8, :] for j in range(lanes)]
        right = [pltpu.roll(core[j], 1, 1) for j in range(lanes)]
        left = [pltpu.roll(core[j], 127, 1) for j in range(lanes)]
        sums = []
        for j in range(lanes):
            west = jnp.where(lane == 0, right[j - 1] if j else 0.0, right[j])
            east = jnp.where(lane == 127, left[j + 1] if j + 1 < lanes else 0.0, left[j])
            north, south = ref[j, at - 1 : at + 7, :], ref[j, at + 1 : at + 9, :]
            sums.append((north + south) + (west + east))
        return core, sums

    def tile_of(ref, i, r, j):
        return ref[i, 8 * r : 8 * r + 8, 128 * j : 128 * j + 128]

    def precision(field, i, year, tiles, finish):
        g = z * YEARS + year
        final = slabs * YEARS - 1
        c = TAU * jnp.where((g > 0) & (g < final), 1.0 + rho * rho, 1.0)
        before = TAU * jnp.where(g > 0, rho, 0.0)
        after = TAU * jnp.where(g < final, rho, 0.0)
        for r in range(4):
            f = inside[r]
            cr, br, ar = (c, before, after) if f is None else (c * f, before * f, after * f)
            for j in range(lanes):
                value = cr * tile_of(field, i, r, j)
                value -= br * tile_of(field, i - 1, r, j) + ar * tile_of(field, i + 1, r, j)
                ys[j, 8 + 8 * r : 16 + 8 * r, :] = value
        for r in range(4):
            core, sums = beside_sum(ys, r)
            for j in range(lanes):
                value = tile_of(k4, 0, r, j) * core[j] - sums[j]
                if inside[r] is not None:
                    value *= inside[r]
                ws[j, 8 + 8 * r : 16 + 8 * r, :] = value
        for r in tiles:
            core, sums = beside_sum(ws, r)
            for j in range(lanes):
                finish(r, j, tile_of(k4, 0, r, j) * core[j] - sums[j])

    for copy in loads[:3]:
        copy.wait()
    pl.semaphore_wait(barrier, len(greeted))
    eta_steps = [[(1, 6 - k, 2 - k), (-1, 1 + k, 5 + k)] for k in (1, 2)]
    eta_near = send_corners(eta, eta_steps[0], 4)
    eta_near += send_whole(eta, eta_steps[0])
    eta_near += send_strips(eta, pl.ds(2, YEARS), 4)
    kappa_strip = send_strips(kappa, 0, 8)
    mask_strip = send_strips(mask, 0, 8)
    eta_far = send_whole(eta, eta_steps[1])
    eta_far += send_corners(eta, eta_steps[1], 4)
    tell(0)
    loads[3].wait()

    arrive(kappa_strip)
    for r in range(4):
        k4[0, 8 * r : 8 * r + 8, :] = kappa[0, 8 * r : 8 * r + 8, :] + 4.0
    arrive(eta_near)
    hear(0)
    tell(1)

    def right_side(year):
        def finish(r, j, value):
            x = tile_of(eta, year + 2, r, j)
            rate = jnp.exp(x)
            sea = tile_of(mask, 0, r, j).astype(jnp.float32)
            caught = counts[year, 8 * r - 8 : 8 * r, 128 * j : 128 * j + 128].astype(jnp.float32)
            new = sea * (caught - rate) - (value + sea * rate * x)
            b[year + 3, 8 * r : 8 * r + 8, 128 * j : 128 * j + 128] = new
            own0[year, 8 * r - 8 : 8 * r, 128 * j : 128 * j + 128] = new

        precision(eta, year + 2, year, (1, 2), finish)

    b_steps = [[(1, 7 - k, 3 - k), (-1, 2 + k, 6 + k)] for k in (1, 2, 3)]
    whole_b, outer_b = [None] * 3, [None] * 3

    def send_b(k):
        whole_b[k] = send_whole(b, b_steps[k])
        outer_b[k] = send_outer(b, b_steps[k], 6)

    @pl.loop(0, 2)
    def _(k):
        right_side(3 * k)

    send_b(0)

    @pl.loop(1, 3)
    def _(k):
        right_side(k)

    b_strips = send_strips(b, pl.ds(3, YEARS), 6)
    send_b(1)
    send_b(2)

    arrive(mask_strip + eta_far)

    @pl.loop(0, YEARS + 4)
    def _(k):
        for r in range(4):
            for j in range(lanes):
                at = (slice(8 * r, 8 * r + 8), slice(128 * j, 128 * j + 128))
                sea = mask[(0, *at)].astype(jnp.float32)
                hess[(k, *at)] = sea * jnp.exp(eta[(k, *at)])

    def power(field, lead, into, into_lead, shift, year, terms=None):
        found = []

        def finish(r, j, value):
            x = tile_of(field, year + lead, r, j)
            new = value + (tile_of(hess, year + 2, r, j) - shift) * x
            if into is v3:
                into[year, 8 * r - 8 : 8 * r, 128 * j : 128 * j + 128] = new
            else:
                into[year + into_lead, 8 * r : 8 * r + 8, 128 * j : 128 * j + 128] = new
            if terms is not None and r in (1, 2):
                if into is not v3:
                    keep = own1 if into is v1 else own2
                    keep[year, 8 * r - 8 : 8 * r, 128 * j : 128 * j + 128] = new
                found.append(terms(x, new, lambda ref, lead: tile_of(ref, year + lead, r, j)))

        precision(field, year + lead, year, (1, 2) if into is v3 else range(4), finish)
        if terms is None:
            return None
        while len(found) > 1:
            found = [tuple(map(jnp.add, p, q)) for p, q in zip(found[::2], found[1::2])]
        return found[0]

    hear(1)
    tell(2)
    first = functools.partial(power, b, 3, v1, 2, SHIFTS[0])
    second = functools.partial(power, v1, 2, v2, 1, SHIFTS[1])
    third = functools.partial(power, v2, 1, v3, 0, SHIFTS[2])

    def receive_b(k):
        arrive(whole_b[k])
        return outer_b[k] + share_inner(b, b_steps[k], 6)

    def own(step, years, terms, count):
        def body(i, sums):
            return tuple(map(jnp.add, sums, step(years(i), terms)))

        return lax.fori_loop(0, 2, body, (zero,) * count)

    edge_years, inner_years = (lambda i: 3 * i), (lambda i: 1 + i)
    terms = lambda x, n, at: (x * x, x * n, n * n)
    both = lambda p, q: tuple(map(jnp.add, p, q))
    first_terms = lambda x, n, at: (x * x, x * n, n * n)
    second_terms = lambda x, n, at: (at(b, 3) * n, x * n, n * n)
    third_terms = lambda x, n, at: (at(v1, 2) * n, x * n)

    corners = receive_b(0)
    arrive(b_strips)
    sums1 = own(first, inner_years, first_terms, 3)
    arrive(corners)
    sums1 = both(sums1, own(first, edge_years, first_terms, 3))
    corners = receive_b(1)
    sums2 = own(second, inner_years, second_terms, 3)
    arrive(corners)

    @pl.loop(0, 2)
    def _(k):
        first(5 * k - 1)

    corners = receive_b(2)
    sums2 = both(sums2, own(second, edge_years, second_terms, 3))
    sums3 = own(third, inner_years, third_terms, 2)
    arrive(corners)

    @pl.loop(0, 2)
    def _(k):
        first(7 * k - 2)

    @pl.loop(0, 2)
    def _(k):
        second(5 * k - 1)

    sums3 = both(sums3, own(third, edge_years, third_terms, 2))
    moments = sums1 + sums2 + sums3
    hear(2)

    row = lax.broadcasted_iota(jnp.int32, (8, 128), 0)
    group = lax.broadcasted_iota(jnp.int32, (8, 128), 1) // 16
    mine = zero
    for k, value in enumerate(moments):
        mine = jnp.where(row == k, jnp.sum(value, axis=0, keepdims=True), mine)
    for shift in (64, 32, 16):
        mine += pltpu.roll(mine, shift, 1)
    mine = jnp.sum(jnp.where(row == group, mine, 0.0), axis=0, keepdims=True)
    for s, (stage, got) in enumerate(zip(stages, (got1, got2))):
        parts[s] = mine
        for i, g in enumerate(stage):
            pltpu.make_async_remote_copy(
                src_ref=parts.at[s],
                dst_ref=got.at[i],
                send_sem=sum_send.at[s],
                recv_sem=sum_recv.at[s],
                device_id=partner(g),
                device_id_type=MESH,
            ).start()
        pltpu.make_async_copy(got, got, sum_recv.at[s]).wait()
        mine += jnp.sum(got[...], axis=0)
    total = jnp.where(row == group, mine, 0.0)
    total = jnp.broadcast_to(jnp.sum(total, axis=1, keepdims=True), (8, 128))
    m00, m01, m11, m02, m12, m22, m13, m23 = [total[k : k + 1, :] for k in range(8)]
    gram = [[m00, m01, m02, m12], [m01, m11, m12, m13], [m02, m12, m22, m23]]

    def product(p, q):
        terms = [a * c * gram[i][j] for i, a in enumerate(p) for j, c in enumerate(q)]
        return functools.reduce(jnp.add, terms)

    def times_q(p):
        return [
            (SHIFTS[i] * p[i] if i < len(p) else 0.0) + (p[i - 1] if i else 0.0)
            for i in range(len(p) + 1)
        ]

    def plus(p, q, scale):
        size = max(len(p), len(q))
        p, q = list(p) + [0.0] * (size - len(p)), list(q) + [0.0] * (size - len(q))
        return [a + scale * c for a, c in zip(p, q)]

    one = jnp.ones((1, 128), jnp.float32)
    step, residual, direction, norm_now = [0.0 * one], [one], [one], m00
    for turn in range(3):
        image = times_q(direction)
        alpha = norm_now / product(direction, image)
        step = plus(step, direction, alpha)
        residual = plus(residual, image, -alpha)
        if turn < 2:
            norm_next = product(residual, residual)
            direction = plus(residual, direction, norm_next / norm_now)
            norm_now = norm_next

    for out, value in zip(weights_out, step + residual):
        for j in range(lanes):
            out[:, 128 * j : 128 * j + 128] = value

    for copy in sent:
        copy.wait_send()
    for s, got in enumerate((got1, got2)):
        pltpu.make_async_copy(got, got, sum_send.at[s]).wait()


def solution(mesh):
    slabs, strips = mesh.shape["year"], mesh.shape["tile"]
    sizes = {"z": slabs, "y": strips // (CHIPS_X * CORES), "x": CHIPS_X, "core": CORES}
    stages = [partners(sizes, ("z", "x")), partners(sizes, ("y", "core"))]
    tokens = [
        reach(sizes, z=(1, -1), y=(1, -1), x=(1, -1)),
        reach(sizes, z=(2, -2), y=(2, -2)),
        reach(sizes, x=(1, -1, 2), core=(1,)),
    ]

    def on_device(eta, counts, mask, kappa2, rho):
        width = eta.shape[-1]
        f32 = jnp.float32
        field = lambda years: pltpu.VMEM((years, TALL, width), f32)
        out = jax.ShapeDtypeStruct(eta.shape, f32)
        args = [pltpu.with_memory_space_constraint(a, pltpu.HBM) for a in (eta, counts, mask, kappa2)]
        v0, v1, v2, v3, *weights = pl.pallas_call(
            functools.partial(kernel, slabs, strips, stages, tokens),
            out_shape=(out,) * 4 + (jax.ShapeDtypeStruct((1, width), f32),) * 7,
            in_specs=[pl.BlockSpec(memory_space=pltpu.HBM)] * 4
            + [pl.BlockSpec(memory_space=pltpu.SMEM)],
            out_specs=(pl.BlockSpec(memory_space=pltpu.VMEM),) * 11,
            scratch_shapes=[
                field(YEARS + 4),
                pltpu.VMEM((YEARS, ROWS, width), jnp.int32),
                pltpu.VMEM((1, TALL, width), jnp.int32),
                field(1),
                field(1),
                field(YEARS + 4),
                field(YEARS + 6),
                field(YEARS + 4),
                field(YEARS + 2),
                pltpu.VMEM((width // 128, TALL + 16, 128), f32),
                pltpu.VMEM((width // 128, TALL + 16, 128), f32),
                pltpu.VMEM((2, 1, 128), f32),
                pltpu.VMEM((len(stages[0]), 1, 128), f32),
                pltpu.VMEM((len(stages[1]), 1, 128), f32),
                pltpu.SemaphoreType.DMA((4,)),
                pltpu.SemaphoreType.DMA((40,)),
                pltpu.SemaphoreType.DMA((40,)),
                pltpu.SemaphoreType.DMA((2,)),
                pltpu.SemaphoreType.DMA((2,)),
                pltpu.SemaphoreType.REGULAR((len(tokens),)),
            ],
            compiler_params=pltpu.CompilerParams(
                collective_id=0, has_side_effects=True, vmem_limit_bytes=40 << 20
            ),
        )(*args, rho)
        of = lambda weights, basis: functools.reduce(jnp.add, map(jnp.multiply, weights, basis))
        return of(weights[:3], (v0, v1, v2)), of(weights[3:], (v0, v1, v2, v3))

    return jax.shard_map(
        on_device,
        mesh=mesh,
        in_specs=(
            P("year", "tile", None),
            P("year", "tile", None),
            P("tile", None),
            P("tile", None),
            P(),
        ),
        out_specs=(P("year", "tile", None),) * 2,
        check_vma=False,
    )
```

```python
import functools
import itertools

import jax
import jax.numpy as jnp
from jax import lax
from jax.experimental import pallas as pl
from jax.experimental.pallas import tpu as pltpu
from jax.sharding import PartitionSpec as P

TAU = 0.05
SHIFTS = (1.0, 6.0, 1.0)
MESH = pl.DeviceIdType.MESH
CHIPS_X, CORES = 4, 2
YEARS, ROWS, EDGE = 4, 16, 8
TALL = ROWS + 2 * EDGE


def around(distance, size):
    return min(distance, size - distance)


def partners(sizes, pick):
    spans = [range(n) if name in pick else range(1) for name, n in sizes.items()]
    found = [g for g in itertools.product(*spans) if any(g)]
    far = lambda g: sum(around(d, n) for d, n in zip(g, sizes.values()))
    return sorted(found, key=lambda g: -far(g))


def reach(sizes, **steps):
    found = []
    for i, (name, n) in enumerate(sizes.items()):
        for step in steps.get(name, ()):
            g = tuple(step % n if k == i else 0 for k in range(len(sizes)))
            if any(g) and g not in found:
                found.append(g)
    return found


def kernel(
    slabs, strips, stages, tokens,
    eta_in, counts_in, mask_in, kappa_in, rho_in, own0, own1, own2, v3, *rest,
):
    *weights_out, eta, counts, mask, kappa, k4, hess, b, v1, v2, ys, ws, kv2 = rest[:19]
    parts, got1, got2, load_sem, send_sem, recv_sem, sum_send, sum_recv, heard = rest[19:]
    z, t = lax.axis_index("year"), lax.axis_index("tile")
    core = lax.rem(t, CORES)
    chips_y = strips // (CHIPS_X * CORES)
    lanes = eta.shape[-1] // 128

    def beside(dz, dt):
        return (lax.rem(z + dz + slabs, slabs), lax.rem(t + dt + strips, strips))

    y, x = t // (CHIPS_X * CORES), lax.rem(t // CORES, CHIPS_X)
    slab_at = [lax.rem(z + d, slabs) for d in range(slabs)]
    row_at = [lax.rem(y + d, chips_y) * (CHIPS_X * CORES) for d in range(chips_y)]
    chip_at = [lax.rem(x + d, CHIPS_X) * CORES for d in range(CHIPS_X)]
    core_at = [core, 1 - core]

    def partner(g):
        dz, dy, dx, dc = g
        return (slab_at[dz], row_at[dy] + (chip_at[dx] + core_at[dc]))

    loads = [
        pltpu.make_async_copy(source, target, load_sem.at[i])
        for i, (source, target) in enumerate(
            [
                (eta_in, eta.at[pl.ds(2, YEARS), pl.ds(EDGE, ROWS)]),
                (kappa_in, kappa.at[0, pl.ds(EDGE, ROWS)]),
                (mask_in, mask.at[0, pl.ds(EDGE, ROWS)]),
                (counts_in, counts),
            ]
        )
    ]
    for copy in loads:
        copy.start()

    barrier = pltpu.get_barrier_semaphore()
    near = [(dz, dt) for dz in (-1, 0, 1) for dt in (-1, 0, 1) if (dz, dt) != (0, 0)]
    greeted = [beside(*n) for n in near] + [partner(g) for g in tokens[0] if not g[0]]
    for device in greeted:
        pl.semaphore_signal(barrier, inc=1, device_id=device, device_id_type=MESH)

    zero = jnp.zeros((8, 128), jnp.float32)
    for j in range(lanes):
        for ref in (ys, ws):
            ref[j, 0:8, :] = zero
            ref[j, 8 + TALL : 16 + TALL, :] = zero
    kv2[0] = jnp.zeros(kv2.shape[1:], jnp.float32)
    for stage, got in zip(stages, (got1, got2)):
        rest_rows = got.shape[0] - len(stage)
        got[len(stage) :, :] = jnp.zeros((rest_rows, 128), jnp.float32)
    rho = rho_in[0]
    top = jnp.where(t > 0, 1.0, 0.0).astype(jnp.float32)
    bottom = jnp.where(t < strips - 1, 1.0, 0.0).astype(jnp.float32)
    inside = (top, None, None, bottom)

    def tell(i):
        for g in tokens[i]:
            pl.semaphore_signal(
                heard.at[i], inc=1, device_id=partner(g), device_id_type=MESH
            )

    def hear(i):
        if tokens[i]:
            pl.semaphore_wait(heard.at[i], len(tokens[i]))

    sent = []

    def remote(*options):
        i = len(sent)
        copies = [
            pltpu.make_async_remote_copy(
                src_ref=source,
                dst_ref=target,
                send_sem=send_sem.at[i],
                recv_sem=recv_sem.at[i],
                device_id=beside(*place),
                device_id_type=MESH,
            )
            for source, target, place in options
        ]
        if len(copies) == 1:
            copies[0].start()
        else:
            for c, copy in enumerate(copies):
                pl.when(core == c)(copy.start)
        sent.append(copies[0])
        return copies[0]

    def arrive(copies):
        for copy in copies:
            copy.wait_recv()

    whole = pl.ds(EDGE, ROWS)

    def down_strip(field, here, there, n, dz):
        source, target = pl.ds(EDGE + ROWS - n, n), pl.ds(EDGE - n, n)
        return field.at[here, source], field.at[there, target], (dz, 1)

    def up_strip(field, here, there, n, dz):
        source, target = pl.ds(EDGE, n), pl.ds(EDGE + ROWS, n)
        return field.at[here, source], field.at[there, target], (dz, -1)

    def send_corners(field, steps, n):
        return [
            remote(strip(field, here, there, n, dz))
            for dz, here, there in steps
            for strip in (down_strip, up_strip)
        ]

    def send_outer(field, steps, n):
        return [
            remote(up_strip(field, here, there, n, dz), down_strip(field, here, there, n, dz))
            for dz, here, there in steps
        ]

    def share_inner(field, steps, n):
        return [
            remote(down_strip(field, there, there, n, 0), up_strip(field, there, there, n, 0))
            for _, _, there in steps
        ]

    def send_whole(field, steps):
        return [
            remote((field.at[here, whole], field.at[there, whole], (dz, 0)))
            for dz, here, there in steps
        ]

    def send_strips(field, years, n):
        return [remote(strip(field, years, years, n, 0)) for strip in (down_strip, up_strip)]

    def beside_sum(ref, r):
        lane = lax.broadcasted_iota(jnp.int32, (8, 128), 1)
        at = 8 + 8 * r
        core = [ref[j, at : at + 8, :] for j in range(lanes)]
        right = [pltpu.roll(core[j], 1, 1) for j in range(lanes)]
        left = [pltpu.roll(core[j], 127, 1) for j in range(lanes)]
        sums = []
        for j in range(lanes):
            west = jnp.where(lane == 0, right[j - 1] if j else 0.0, right[j])
            east = jnp.where(lane == 127, left[j + 1] if j + 1 < lanes else 0.0, left[j])
            north, south = ref[j, at - 1 : at + 7, :], ref[j, at + 1 : at + 9, :]
            sums.append((north + south) + (west + east))
        return core, sums

    def tile_of(ref, i, r, j):
        return ref[i, 8 * r : 8 * r + 8, 128 * j : 128 * j + 128]

    def precision(field, i, year, tiles, finish):
        g = z * YEARS + year
        final = slabs * YEARS - 1
        c = TAU * jnp.where((g > 0) & (g < final), 1.0 + rho * rho, 1.0)
        before = TAU * jnp.where(g > 0, rho, 0.0)
        after = TAU * jnp.where(g < final, rho, 0.0)
        for r in range(4):
            f = inside[r]
            cr, br, ar = (c, before, after) if f is None else (c * f, before * f, after * f)
            for j in range(lanes):
                value = cr * tile_of(field, i, r, j)
                value -= br * tile_of(field, i - 1, r, j) + ar * tile_of(field, i + 1, r, j)
                ys[j, 8 + 8 * r : 16 + 8 * r, :] = value
        for r in range(4):
            core, sums = beside_sum(ys, r)
            for j in range(lanes):
                value = tile_of(k4, 0, r, j) * core[j] - sums[j]
                if inside[r] is not None:
                    value *= inside[r]
                ws[j, 8 + 8 * r : 16 + 8 * r, :] = value
        for r in tiles:
            core, sums = beside_sum(ws, r)
            for j in range(lanes):
                finish(r, j, tile_of(k4, 0, r, j) * core[j] - sums[j])

    for copy in loads[:3]:
        copy.wait()
    pl.semaphore_wait(barrier, len(greeted))
    eta_steps = [[(1, 6 - k, 2 - k), (-1, 1 + k, 5 + k)] for k in (1, 2)]
    eta_near = send_corners(eta, eta_steps[0], 4)
    eta_near += send_whole(eta, eta_steps[0])
    eta_near += send_strips(eta, pl.ds(2, YEARS), 4)
    kappa_strip = send_strips(kappa, 0, 8)
    mask_strip = send_strips(mask, 0, 8)
    eta_far = send_whole(eta, eta_steps[1])
    eta_far += send_corners(eta, eta_steps[1], 4)
    tell(0)
    loads[3].wait()

    arrive(kappa_strip)
    for r in range(4):
        k4[0, 8 * r : 8 * r + 8, :] = kappa[0, 8 * r : 8 * r + 8, :] + 4.0
    arrive(eta_near)
    hear(0)
    tell(1)

    def right_side(year):
        def finish(r, j, value):
            x = tile_of(eta, year + 2, r, j)
            rate = jnp.exp(x)
            sea = tile_of(mask, 0, r, j).astype(jnp.float32)
            caught = counts[year, 8 * r - 8 : 8 * r, 128 * j : 128 * j + 128].astype(jnp.float32)
            new = sea * (caught - rate) - (value + sea * rate * x)
            b[year + 3, 8 * r : 8 * r + 8, 128 * j : 128 * j + 128] = new
            own0[year, 8 * r - 8 : 8 * r, 128 * j : 128 * j + 128] = new

        precision(eta, year + 2, year, (1, 2), finish)

    b_steps = [[(1, 7 - k, 3 - k), (-1, 2 + k, 6 + k)] for k in (1, 2, 3)]
    whole_b, outer_b = [None] * 3, [None] * 3

    def send_b(k):
        whole_b[k] = send_whole(b, b_steps[k])
        outer_b[k] = send_outer(b, b_steps[k], 6)

    @pl.loop(0, 2)
    def _(k):
        right_side(3 * k)

    send_b(0)

    @pl.loop(1, 3)
    def _(k):
        right_side(k)

    b_strips = send_strips(b, pl.ds(3, YEARS), 6)
    send_b(1)
    send_b(2)

    arrive(mask_strip + eta_far)

    @pl.loop(0, YEARS + 4)
    def _(k):
        for r in range(4):
            for j in range(lanes):
                at = (slice(8 * r, 8 * r + 8), slice(128 * j, 128 * j + 128))
                sea = mask[(0, *at)].astype(jnp.float32)
                hess[(k, *at)] = sea * jnp.exp(eta[(k, *at)])

    def power(field, lead, into, into_lead, shift, year, terms=None):
        found = []

        def finish(r, j, value):
            x = tile_of(field, year + lead, r, j)
            new = value + (tile_of(hess, year + 2, r, j) - shift) * x
            if into is v3:
                into[year, 8 * r - 8 : 8 * r, 128 * j : 128 * j + 128] = new
            else:
                into[year + into_lead, 8 * r : 8 * r + 8, 128 * j : 128 * j + 128] = new
            if terms is not None and r in (1, 2):
                if into is not v3:
                    keep = own1 if into is v1 else own2
                    keep[year, 8 * r - 8 : 8 * r, 128 * j : 128 * j + 128] = new
                found.append(terms(x, new, lambda ref, lead: tile_of(ref, year + lead, r, j)))

        precision(field, year + lead, year, (1, 2) if into is v3 else range(4), finish)
        if terms is None:
            return None
        while len(found) > 1:
            found = [tuple(map(jnp.add, p, q)) for p, q in zip(found[::2], found[1::2])]
        return found[0]

    hear(1)
    tell(2)
    first = functools.partial(power, b, 3, v1, 2, SHIFTS[0])
    second = functools.partial(power, v1, 2, v2, 1, SHIFTS[1])
    third = functools.partial(power, v2, 1, v3, 0, SHIFTS[2])

    def receive_b(k, ways=slice(None)):
        arrive(whole_b[k][ways])
        return outer_b[k][ways] + share_inner(b, b_steps[k][ways], 6)

    def own(step, years, terms, count):
        def body(i, sums):
            return tuple(map(jnp.add, sums, step(years(i), terms)))

        return lax.fori_loop(0, 2, body, (zero,) * count)

    edge_years, inner_years = (lambda i: 3 * i), (lambda i: 1 + i)
    terms = lambda x, n, at: (x * x, x * n, n * n)
    both = lambda p, q: tuple(map(jnp.add, p, q))
    first_terms = lambda x, n, at: (x * x, x * n, n * n)
    second_terms = lambda x, n, at: (at(b, 3) * n, x * n, n * n)

    def energy(year, own):
        g = z * YEARS + year
        final = slabs * YEARS - 1
        c = TAU * jnp.where((g > 0) & (g < final), 1.0 + rho * rho, 1.0)
        link = 2.0 * TAU * jnp.where(g <= final, rho, 0.0)
        for r in range(4):
            for j in range(lanes):
                x = tile_of(v2, year + 1, r, j)
                ys[j, 8 + 8 * r : 16 + 8 * r, :] = x if inside[r] is None else inside[r] * x
        found = []
        for r in (1, 2):
            core, sums = beside_sum(ys, r)
            for j in range(lanes):
                at = (slice(8 * r - 8, 8 * r), slice(128 * j, 128 * j + 128))
                w = tile_of(k4, 0, r, j) * core[j] - sums[j]
                value = -link * kv2[(year, *at)]
                if own:
                    value += c * w
                    kv2[(year + 1, *at)] = w
                value *= w
                if own:
                    x = tile_of(v2, year + 1, r, j)
                    value += (tile_of(hess, year + 2, r, j) - SHIFTS[2]) * (x * x)
                found.append(value)
        while len(found) > 1:
            found = [p + q for p, q in zip(found[::2], found[1::2])]
        return found[0]

    corners = receive_b(0)
    arrive(b_strips)
    sums1 = own(first, inner_years, first_terms, 3)
    arrive(corners)
    sums1 = both(sums1, own(first, edge_years, first_terms, 3))
    corners = receive_b(1)
    hear(2)
    tell(3)
    sums2 = own(second, inner_years, second_terms, 3)
    arrive(corners)

    @pl.loop(0, 2)
    def _(k):
        first(5 * k - 1)

    corners = receive_b(2, slice(1, 2))
    sums2 = both(sums2, own(second, edge_years, second_terms, 3))
    sums3 = lax.fori_loop(0, YEARS, lambda year, found: found + energy(year, True), zero)
    arrive(corners)
    first(YEARS + 1)
    second(YEARS)
    moments = sums1 + sums2 + (sums3 + energy(YEARS, False),)
    hear(3)

    def finish_basis():
        corners = receive_b(2, slice(0, 1))

        @pl.loop(1, 3)
        def _(k):
            third(k)

        arrive(corners)
        first(-2)
        second(-1)

        @pl.loop(0, 2)
        def _(k):
            third(3 * k)

    row = lax.broadcasted_iota(jnp.int32, (8, 128), 0)
    group = lax.broadcasted_iota(jnp.int32, (8, 128), 1) // 16
    mine = zero
    for k, value in enumerate(moments):
        mine = jnp.where(row == k, jnp.sum(value, axis=0, keepdims=True), mine)
    for shift in (64, 32, 16):
        mine += pltpu.roll(mine, shift, 1)
    mine = jnp.sum(jnp.where(row == group, mine, 0.0), axis=0, keepdims=True)
    for s, (stage, got) in enumerate(zip(stages, (got1, got2))):
        parts[s] = mine
        for i, g in enumerate(stage):
            pltpu.make_async_remote_copy(
                src_ref=parts.at[s],
                dst_ref=got.at[pl.ds(i, 1)],
                send_sem=sum_send.at[s],
                recv_sem=sum_recv.at[s],
                device_id=partner(g),
                device_id_type=MESH,
            ).start()
        if s == len(stages) - 1:
            finish_basis()
        landed = got.at[pl.ds(0, len(stage))]
        pltpu.make_async_copy(landed, landed, sum_recv.at[s]).wait()
        mine += jnp.sum(got[...], axis=0, keepdims=True)
    total = jnp.where(row == group, mine, 0.0)
    total = jnp.broadcast_to(jnp.sum(total, axis=1, keepdims=True), (8, 128))
    m00, m01, m11, m02, m12, m22, m23 = [total[k : k + 1, :] for k in range(7)]
    m13 = m22 + (SHIFTS[1] - SHIFTS[2]) * m12
    gram = [[m00, m01, m02, m12], [m01, m11, m12, m13], [m02, m12, m22, m23]]

    def product(p, q):
        terms = [a * c * gram[i][j] for i, a in enumerate(p) for j, c in enumerate(q)]
        while len(terms) > 1:
            terms = [sum(terms[k : k + 2]) for k in range(0, len(terms), 2)]
        return terms[0]

    def times_q(p):
        return [
            (SHIFTS[i] * p[i] if i < len(p) else 0.0) + (p[i - 1] if i else 0.0)
            for i in range(len(p) + 1)
        ]

    def plus(p, q, scale):
        size = max(len(p), len(q))
        p, q = list(p) + [0.0] * (size - len(p)), list(q) + [0.0] * (size - len(q))
        return [a + scale * c for a, c in zip(p, q)]

    one = jnp.ones((1, 128), jnp.float32)
    step, residual, direction, norm_now = [0.0 * one], [one], [one], m00
    for turn in range(3):
        image = times_q(direction)
        alpha = norm_now / product(direction, image)
        step = plus(step, direction, alpha)
        residual = plus(residual, image, -alpha)
        if turn < 2:
            norm_next = product(residual, residual)
            direction = plus(residual, direction, norm_next / norm_now)
            norm_now = norm_next

    for out, value in zip(weights_out, step + residual):
        for j in range(lanes):
            out[:, 128 * j : 128 * j + 128] = value

    for copy in sent:
        copy.wait_send()
    for s, (stage, got) in enumerate(zip(stages, (got1, got2))):
        landed = got.at[pl.ds(0, len(stage))]
        pltpu.make_async_copy(landed, landed, sum_send.at[s]).wait()


def solution(mesh):
    slabs, strips = mesh.shape["year"], mesh.shape["tile"]
    sizes = {"z": slabs, "y": strips // (CHIPS_X * CORES), "x": CHIPS_X, "core": CORES}
    stages = [partners(sizes, ("core",)), partners(sizes, ("z", "y", "x"))]
    tokens = [
        reach(sizes, z=(1, -1), y=(1, -1), x=(1, -1)),
        reach(sizes, z=(2, -2), y=(2, -2)),
        reach(sizes, x=(1, -1, 2)),
        reach(sizes, y=range(1, sizes["y"])),
    ]

    def on_device(eta, counts, mask, kappa2, rho):
        width = eta.shape[-1]
        f32 = jnp.float32
        field = lambda years: pltpu.VMEM((years, TALL, width), f32)
        out = jax.ShapeDtypeStruct(eta.shape, f32)
        args = [pltpu.with_memory_space_constraint(a, pltpu.HBM) for a in (eta, counts, mask, kappa2)]
        v0, v1, v2, v3, *weights = pl.pallas_call(
            functools.partial(kernel, slabs, strips, stages, tokens),
            out_shape=(out,) * 4 + (jax.ShapeDtypeStruct((1, width), f32),) * 7,
            in_specs=[pl.BlockSpec(memory_space=pltpu.HBM)] * 4
            + [pl.BlockSpec(memory_space=pltpu.SMEM)],
            out_specs=(pl.BlockSpec(memory_space=pltpu.VMEM),) * 11,
            scratch_shapes=[
                field(YEARS + 4),
                pltpu.VMEM((YEARS, ROWS, width), jnp.int32),
                pltpu.VMEM((1, TALL, width), jnp.int32),
                field(1),
                field(1),
                field(YEARS + 4),
                field(YEARS + 6),
                field(YEARS + 4),
                field(YEARS + 2),
                pltpu.VMEM((width // 128, TALL + 16, 128), f32),
                pltpu.VMEM((width // 128, TALL + 16, 128), f32),
                pltpu.VMEM((YEARS + 1, ROWS, width), f32),
                pltpu.VMEM((2, 1, 128), f32),
                pltpu.VMEM((len(stages[0]) // 8 * 8 + 8, 128), f32),
                pltpu.VMEM((len(stages[1]) // 8 * 8 + 8, 128), f32),
                pltpu.SemaphoreType.DMA((4,)),
                pltpu.SemaphoreType.DMA((40,)),
                pltpu.SemaphoreType.DMA((40,)),
                pltpu.SemaphoreType.DMA((2,)),
                pltpu.SemaphoreType.DMA((2,)),
                pltpu.SemaphoreType.REGULAR((len(tokens),)),
            ],
            compiler_params=pltpu.CompilerParams(
                collective_id=0, has_side_effects=True, vmem_limit_bytes=40 << 20
            ),
        )(*args, rho)
        of = lambda weights, basis: functools.reduce(jnp.add, map(jnp.multiply, weights, basis))
        return of(weights[:3], (v0, v1, v2)), of(weights[3:], (v0, v1, v2, v3))

    return jax.shard_map(
        on_device,
        mesh=mesh,
        in_specs=(
            P("year", "tile", None),
            P("year", "tile", None),
            P("tile", None),
            P("tile", None),
            P(),
        ),
        out_specs=(P("year", "tile", None),) * 2,
        check_vma=False,
    )
```

```python
import functools
import itertools

import jax
import jax.numpy as jnp
from jax import lax
from jax.experimental import pallas as pl
from jax.experimental.pallas import tpu as pltpu
from jax.sharding import PartitionSpec as P

TAU = 0.05
SHIFTS = (1.0, 6.0, 1.0)
MESH = pl.DeviceIdType.MESH
CHIPS_X, CORES = 4, 2
YEARS, ROWS, EDGE = 4, 16, 8
TALL = ROWS + 2 * EDGE


def around(distance, size):
    return min(distance, size - distance)


def partners(sizes, pick):
    spans = [range(n) if name in pick else range(1) for name, n in sizes.items()]
    found = [g for g in itertools.product(*spans) if any(g)]
    far = lambda g: sum(around(d, n) for d, n in zip(g, sizes.values()))
    return sorted(found, key=lambda g: -far(g))


def reach(sizes, **steps):
    found = []
    for i, (name, n) in enumerate(sizes.items()):
        for step in steps.get(name, ()):
            g = tuple(step % n if k == i else 0 for k in range(len(sizes)))
            if any(g) and g not in found:
                found.append(g)
    return found


def kernel(
    slabs, strips, stages, tokens,
    eta_in, counts_in, mask_in, kappa_in, rho_in, own0, own1, own2, v3, *rest,
):
    *weights_out, eta, counts, mask, kappa, k4, hess, b, v1, v2, y0, y1, w0, w1, kv2 = rest[:21]
    ys, ws = (y0, y1), (w0, w1)
    parts, got1, got2, load_sem, send_sem, recv_sem, sum_send, sum_recv, heard = rest[21:]
    z, t = lax.axis_index("year"), lax.axis_index("tile")
    core = lax.rem(t, CORES)
    chips_y = strips // (CHIPS_X * CORES)
    lanes = eta.shape[-1] // 128

    def beside(dz, dt):
        return (lax.rem(z + dz + slabs, slabs), lax.rem(t + dt + strips, strips))

    y, x = t // (CHIPS_X * CORES), lax.rem(t // CORES, CHIPS_X)
    slab_at = [lax.rem(z + d, slabs) for d in range(slabs)]
    row_at = [lax.rem(y + d, chips_y) * (CHIPS_X * CORES) for d in range(chips_y)]
    chip_at = [lax.rem(x + d, CHIPS_X) * CORES for d in range(CHIPS_X)]
    core_at = [core, 1 - core]

    def partner(g):
        dz, dy, dx, dc = g
        return (slab_at[dz], row_at[dy] + (chip_at[dx] + core_at[dc]))

    loads = [
        pltpu.make_async_copy(source, target, load_sem.at[i])
        for i, (source, target) in enumerate(
            [
                (eta_in, eta.at[pl.ds(2, YEARS), pl.ds(EDGE, ROWS)]),
                (kappa_in, kappa.at[0, pl.ds(EDGE, ROWS)]),
                (mask_in, mask.at[0, pl.ds(EDGE, ROWS)]),
                (counts_in, counts),
            ]
        )
    ]
    for copy in loads:
        copy.start()

    barrier = pltpu.get_barrier_semaphore()
    near = [(dz, dt) for dz in (-1, 0, 1) for dt in (-1, 0, 1) if (dz, dt) != (0, 0)]
    greeted = [beside(*n) for n in near] + [partner(g) for g in tokens[0] if not g[0]]
    for device in greeted:
        pl.semaphore_signal(barrier, inc=1, device_id=device, device_id_type=MESH)

    zero = jnp.zeros((8, 128), jnp.float32)
    for j in range(lanes):
        for ref in (*ys, *ws):
            ref[j, 0:8, :] = zero
            ref[j, 8 + TALL : 16 + TALL, :] = zero
    for stage, got in zip(stages, (got1, got2)):
        rest_rows = got.shape[0] - len(stage)
        got[len(stage) :, :] = jnp.zeros((rest_rows, 128), jnp.float32)
    rho = rho_in[0]
    top = jnp.where(t > 0, 1.0, 0.0).astype(jnp.float32)
    bottom = jnp.where(t < strips - 1, 1.0, 0.0).astype(jnp.float32)
    inside = (top, None, None, bottom)

    def tell(i):
        for g in tokens[i]:
            pl.semaphore_signal(
                heard.at[i], inc=1, device_id=partner(g), device_id_type=MESH
            )

    def hear(i):
        if tokens[i]:
            pl.semaphore_wait(heard.at[i], len(tokens[i]))

    sent = []

    def remote(*options):
        i = len(sent)
        copies = [
            pltpu.make_async_remote_copy(
                src_ref=source,
                dst_ref=target,
                send_sem=send_sem.at[i],
                recv_sem=recv_sem.at[i],
                device_id=beside(*place),
                device_id_type=MESH,
            )
            for source, target, place in options
        ]
        if len(copies) == 1:
            copies[0].start()
        else:
            for c, copy in enumerate(copies):
                pl.when(core == c)(copy.start)
        sent.append(copies[0])
        return copies[0]

    def arrive(copies):
        for copy in copies:
            copy.wait_recv()

    whole = pl.ds(EDGE, ROWS)

    def down_strip(field, here, there, n, dz):
        source, target = pl.ds(EDGE + ROWS - n, n), pl.ds(EDGE - n, n)
        return field.at[here, source], field.at[there, target], (dz, 1)

    def up_strip(field, here, there, n, dz):
        source, target = pl.ds(EDGE, n), pl.ds(EDGE + ROWS, n)
        return field.at[here, source], field.at[there, target], (dz, -1)

    def send_corners(field, steps, n):
        return [
            remote(strip(field, here, there, n, dz))
            for dz, here, there in steps
            for strip in (down_strip, up_strip)
        ]

    def send_outer(field, steps, n):
        return [
            remote(up_strip(field, here, there, n, dz), down_strip(field, here, there, n, dz))
            for dz, here, there in steps
        ]

    def share_inner(field, steps, n):
        return [
            remote(down_strip(field, there, there, n, 0), up_strip(field, there, there, n, 0))
            for _, _, there in steps
        ]

    def send_whole(field, steps):
        return [
            remote((field.at[here, whole], field.at[there, whole], (dz, 0)))
            for dz, here, there in steps
        ]

    def send_strips(field, years, n):
        return [remote(strip(field, years, years, n, 0)) for strip in (down_strip, up_strip)]

    def beside_sum(ref, r):
        lane = lax.broadcasted_iota(jnp.int32, (8, 128), 1)
        at = 8 + 8 * r
        core = [ref[j, at : at + 8, :] for j in range(lanes)]
        right = [pltpu.roll(core[j], 1, 1) for j in range(lanes)]
        left = [pltpu.roll(core[j], 127, 1) for j in range(lanes)]
        sums = []
        for j in range(lanes):
            west = jnp.where(lane == 0, right[j - 1] if j else 0.0, right[j])
            east = jnp.where(lane == 127, left[j + 1] if j + 1 < lanes else 0.0, left[j])
            north, south = ref[j, at - 1 : at + 7, :], ref[j, at + 1 : at + 9, :]
            sums.append((north + south) + (west + east))
        return core, sums

    def tile_of(ref, i, r, j):
        return ref[i, 8 * r : 8 * r + 8, 128 * j : 128 * j + 128]

    def precision(field, tiles, jobs):
        final = slabs * YEARS - 1
        for r in range(4):
            f = inside[r]
            for n, (i, year, _) in enumerate(jobs):
                g = z * YEARS + year
                c = TAU * jnp.where((g > 0) & (g < final), 1.0 + rho * rho, 1.0)
                before = TAU * jnp.where(g > 0, rho, 0.0)
                after = TAU * jnp.where(g < final, rho, 0.0)
                if f is not None:
                    c, before, after = c * f, before * f, after * f
                for j in range(lanes):
                    value = c * tile_of(field, i, r, j)
                    value -= before * tile_of(field, i - 1, r, j) + after * tile_of(field, i + 1, r, j)
                    ys[n][j, 8 + 8 * r : 16 + 8 * r, :] = value
        for r in range(4):
            for n in range(len(jobs)):
                core, sums = beside_sum(ys[n], r)
                for j in range(lanes):
                    value = tile_of(k4, 0, r, j) * core[j] - sums[j]
                    if inside[r] is not None:
                        value *= inside[r]
                    ws[n][j, 8 + 8 * r : 16 + 8 * r, :] = value
        for r in tiles:
            for n, (_, _, finish) in enumerate(jobs):
                core, sums = beside_sum(ws[n], r)
                for j in range(lanes):
                    finish(r, j, tile_of(k4, 0, r, j) * core[j] - sums[j])

    for copy in loads[:3]:
        copy.wait()
    pl.semaphore_wait(barrier, len(greeted))
    eta_steps = [[(1, 6 - k, 2 - k), (-1, 1 + k, 5 + k)] for k in (1, 2)]
    eta_near = send_corners(eta, eta_steps[0], 4)
    eta_near += send_whole(eta, eta_steps[0])
    eta_near += send_strips(eta, pl.ds(2, YEARS), 4)
    kappa_strip = send_strips(kappa, 0, 8)
    mask_strip = send_strips(mask, 0, 8)
    eta_far = send_whole(eta, eta_steps[1])
    eta_far += send_corners(eta, eta_steps[1], 4)
    tell(0)
    loads[3].wait()

    arrive(kappa_strip)
    for r in range(4):
        k4[0, 8 * r : 8 * r + 8, :] = kappa[0, 8 * r : 8 * r + 8, :] + 4.0
    arrive(eta_near)
    hear(0)
    tell(1)

    def right_side(years):
        def finish(year, r, j, value):
            x = tile_of(eta, year + 2, r, j)
            rate = jnp.exp(x)
            sea = tile_of(mask, 0, r, j).astype(jnp.float32)
            caught = counts[year, 8 * r - 8 : 8 * r, 128 * j : 128 * j + 128].astype(jnp.float32)
            new = sea * (caught - rate) - (value + sea * rate * x)
            b[year + 3, 8 * r : 8 * r + 8, 128 * j : 128 * j + 128] = new
            own0[year, 8 * r - 8 : 8 * r, 128 * j : 128 * j + 128] = new

        jobs = [(year + 2, year, functools.partial(finish, year)) for year in years]
        precision(eta, (1, 2), jobs)

    b_steps = [[(1, 7 - k, 3 - k), (-1, 2 + k, 6 + k)] for k in (1, 2, 3)]
    whole_b, outer_b = [None] * 3, [None] * 3

    def send_b(k):
        whole_b[k] = send_whole(b, b_steps[k])
        outer_b[k] = send_outer(b, b_steps[k], 6)

    right_side((0, 3))
    send_b(0)

    right_side((1, 2))
    b_strips = send_strips(b, pl.ds(3, YEARS), 6)
    send_b(1)
    send_b(2)

    arrive(mask_strip + eta_far)

    @pl.loop(0, YEARS + 4)
    def _(k):
        for r in range(4):
            for j in range(lanes):
                at = (slice(8 * r, 8 * r + 8), slice(128 * j, 128 * j + 128))
                sea = mask[(0, *at)].astype(jnp.float32)
                hess[(k, *at)] = sea * jnp.exp(eta[(k, *at)])

    def power(field, lead, into, into_lead, shift, years, terms=None):
        found = []

        def finish(year, r, j, value):
            x = tile_of(field, year + lead, r, j)
            new = value + (tile_of(hess, year + 2, r, j) - shift) * x
            if into is v3:
                into[year, 8 * r - 8 : 8 * r, 128 * j : 128 * j + 128] = new
            else:
                into[year + into_lead, 8 * r : 8 * r + 8, 128 * j : 128 * j + 128] = new
            if terms is not None and r in (1, 2):
                if into is not v3:
                    keep = own1 if into is v1 else own2
                    keep[year, 8 * r - 8 : 8 * r, 128 * j : 128 * j + 128] = new
                found.append(terms(x, new, lambda ref, lead: tile_of(ref, year + lead, r, j)))

        jobs = [(year + lead, year, functools.partial(finish, year)) for year in years]
        precision(field, (1, 2) if into is v3 else range(4), jobs)
        if terms is None:
            return None
        while len(found) > 1:
            found = [tuple(map(jnp.add, p, q)) for p, q in zip(found[::2], found[1::2])]
        return found[0]

    hear(1)
    tell(2)
    first = functools.partial(power, b, 3, v1, 2, SHIFTS[0])
    second = functools.partial(power, v1, 2, v2, 1, SHIFTS[1])
    third = functools.partial(power, v2, 1, v3, 0, SHIFTS[2])

    def receive_b(k, ways=slice(None)):
        arrive(whole_b[k][ways])
        return outer_b[k][ways] + share_inner(b, b_steps[k][ways], 6)

    edge_years, inner_years = (0, 3), (1, 2)
    both = lambda p, q: tuple(map(jnp.add, p, q))
    first_terms = lambda x, n, at: (x * x, x * n, n * n)
    second_terms = lambda x, n, at: (at(b, 3) * n, x * n, n * n)

    def energy(year, links, own=True):
        g = z * YEARS + year
        final = slabs * YEARS - 1
        c = TAU * jnp.where((g > 0) & (g < final), 1.0 + rho * rho, 1.0)
        link = 2.0 * TAU * jnp.where(g <= final, rho, 0.0)
        rows = ys[year % 2]
        for r in range(4):
            for j in range(lanes):
                x = tile_of(v2, year + 1, r, j)
                rows[j, 8 + 8 * r : 16 + 8 * r, :] = x if inside[r] is None else inside[r] * x
        found = []
        for r in (1, 2):
            core, sums = beside_sum(rows, r)
            for j in range(lanes):
                at = (slice(8 * r - 8, 8 * r), slice(128 * j, 128 * j + 128))
                w = tile_of(k4, 0, r, j) * core[j] - sums[j]
                value = c * w if own else zero
                for other in links:
                    value -= link * kv2[(other, *at)]
                value *= w
                if own:
                    kv2[(year, *at)] = w
                    x = tile_of(v2, year + 1, r, j)
                    value += (tile_of(hess, year + 2, r, j) - SHIFTS[2]) * (x * x)
                found.append(value)
        while len(found) > 1:
            found = [p + q for p, q in zip(found[::2], found[1::2])]
        return found[0]

    corners = receive_b(0)
    arrive(b_strips)
    sums1 = first(inner_years, first_terms)
    arrive(corners)
    sums1 = both(sums1, first(edge_years, first_terms))
    corners = receive_b(1)
    hear(2)
    tell(3)
    sums2 = second(inner_years, second_terms)
    sums3 = energy(1, ()) + energy(2, (1,))
    arrive(corners)

    first((-1, 4))

    corners = receive_b(2, slice(1, 2))
    sums2 = both(sums2, second(edge_years, second_terms))
    sums3 += energy(0, (1,)) + energy(3, (2,))
    arrive(corners)
    first((YEARS + 1,))
    second((YEARS,))
    moments = sums1 + sums2 + (sums3 + energy(YEARS, (3,), own=False),)
    hear(3)

    def finish_basis():
        corners = receive_b(2, slice(0, 1))
        third(inner_years)
        arrive(corners)
        first((-2,))
        second((-1,))
        third(edge_years)

    row = lax.broadcasted_iota(jnp.int32, (8, 128), 0)
    group = lax.broadcasted_iota(jnp.int32, (8, 128), 1) // 16
    mine = zero
    for k, value in enumerate(moments):
        mine = jnp.where(row == k, jnp.sum(value, axis=0, keepdims=True), mine)
    for shift in (64, 32, 16):
        mine += pltpu.roll(mine, shift, 1)
    mine = jnp.sum(jnp.where(row == group, mine, 0.0), axis=0, keepdims=True)
    for s, (stage, got) in enumerate(zip(stages, (got1, got2))):
        parts[s] = mine
        for i, g in enumerate(stage):
            pltpu.make_async_remote_copy(
                src_ref=parts.at[s],
                dst_ref=got.at[pl.ds(i, 1)],
                send_sem=sum_send.at[s],
                recv_sem=sum_recv.at[s],
                device_id=partner(g),
                device_id_type=MESH,
            ).start()
        if s == len(stages) - 1:
            finish_basis()
        landed = got.at[pl.ds(0, len(stage))]
        pltpu.make_async_copy(landed, landed, sum_recv.at[s]).wait()
        mine += jnp.sum(got[...], axis=0, keepdims=True)
    total = jnp.where(row == group, mine, 0.0)
    total = jnp.broadcast_to(jnp.sum(total, axis=1, keepdims=True), (8, 128))
    m00, m01, m11, m02, m12, m22, m23 = [total[k : k + 1, :] for k in range(7)]
    m13 = m22 + (SHIFTS[1] - SHIFTS[2]) * m12
    gram = [[m00, m01, m02, m12], [m01, m11, m12, m13], [m02, m12, m22, m23]]

    def product(p, q):
        terms = [a * c * gram[i][j] for i, a in enumerate(p) for j, c in enumerate(q)]
        while len(terms) > 1:
            terms = [sum(terms[k : k + 2]) for k in range(0, len(terms), 2)]
        return terms[0]

    def times_q(p):
        return [
            (SHIFTS[i] * p[i] if i < len(p) else 0.0) + (p[i - 1] if i else 0.0)
            for i in range(len(p) + 1)
        ]

    def plus(p, q, scale):
        size = max(len(p), len(q))
        p, q = list(p) + [0.0] * (size - len(p)), list(q) + [0.0] * (size - len(q))
        return [a + scale * c for a, c in zip(p, q)]

    one = jnp.ones((1, 128), jnp.float32)
    step, residual, direction, norm_now = [0.0 * one], [one], [one], m00
    for turn in range(3):
        image = times_q(direction)
        alpha = norm_now / product(direction, image)
        step = plus(step, direction, alpha)
        residual = plus(residual, image, -alpha)
        if turn < 2:
            norm_next = product(residual, residual)
            direction = plus(residual, direction, norm_next / norm_now)
            norm_now = norm_next

    for out, value in zip(weights_out, step + residual):
        for j in range(lanes):
            out[:, 128 * j : 128 * j + 128] = value

    for copy in sent:
        copy.wait_send()
    for s, (stage, got) in enumerate(zip(stages, (got1, got2))):
        landed = got.at[pl.ds(0, len(stage))]
        pltpu.make_async_copy(landed, landed, sum_send.at[s]).wait()


def solution(mesh):
    slabs, strips = mesh.shape["year"], mesh.shape["tile"]
    sizes = {"z": slabs, "y": strips // (CHIPS_X * CORES), "x": CHIPS_X, "core": CORES}
    stages = [partners(sizes, ("core",)), partners(sizes, ("z", "y", "x"))]
    tokens = [
        reach(sizes, z=(1, -1), y=(1, -1), x=(1, -1)),
        reach(sizes, z=(2, -2), y=(2, -2)),
        reach(sizes, x=(1, -1, 2)),
        reach(sizes, y=range(1, sizes["y"])),
    ]

    def on_device(eta, counts, mask, kappa2, rho):
        width = eta.shape[-1]
        f32 = jnp.float32
        field = lambda years: pltpu.VMEM((years, TALL, width), f32)
        out = jax.ShapeDtypeStruct(eta.shape, f32)
        args = [pltpu.with_memory_space_constraint(a, pltpu.HBM) for a in (eta, counts, mask, kappa2)]
        v0, v1, v2, v3, *weights = pl.pallas_call(
            functools.partial(kernel, slabs, strips, stages, tokens),
            out_shape=(out,) * 4 + (jax.ShapeDtypeStruct((1, width), f32),) * 7,
            in_specs=[pl.BlockSpec(memory_space=pltpu.HBM)] * 4
            + [pl.BlockSpec(memory_space=pltpu.SMEM)],
            out_specs=(pl.BlockSpec(memory_space=pltpu.VMEM),) * 11,
            scratch_shapes=[
                field(YEARS + 4),
                pltpu.VMEM((YEARS, ROWS, width), jnp.int32),
                pltpu.VMEM((1, TALL, width), jnp.int32),
                field(1),
                field(1),
                field(YEARS + 4),
                field(YEARS + 6),
                field(YEARS + 4),
                field(YEARS + 2),
                pltpu.VMEM((width // 128, TALL + 16, 128), f32),
                pltpu.VMEM((width // 128, TALL + 16, 128), f32),
                pltpu.VMEM((width // 128, TALL + 16, 128), f32),
                pltpu.VMEM((width // 128, TALL + 16, 128), f32),
                pltpu.VMEM((YEARS, ROWS, width), f32),
                pltpu.VMEM((2, 1, 128), f32),
                pltpu.VMEM((len(stages[0]) // 8 * 8 + 8, 128), f32),
                pltpu.VMEM((len(stages[1]) // 8 * 8 + 8, 128), f32),
                pltpu.SemaphoreType.DMA((4,)),
                pltpu.SemaphoreType.DMA((40,)),
                pltpu.SemaphoreType.DMA((40,)),
                pltpu.SemaphoreType.DMA((2,)),
                pltpu.SemaphoreType.DMA((2,)),
                pltpu.SemaphoreType.REGULAR((len(tokens),)),
            ],
            compiler_params=pltpu.CompilerParams(
                collective_id=0, has_side_effects=True, vmem_limit_bytes=40 << 20
            ),
        )(*args, rho)
        of = lambda weights, basis: functools.reduce(jnp.add, map(jnp.multiply, weights, basis))
        return of(weights[:3], (v0, v1, v2)), of(weights[3:], (v0, v1, v2, v3))

    return jax.shard_map(
        on_device,
        mesh=mesh,
        in_specs=(
            P("year", "tile", None),
            P("year", "tile", None),
            P("tile", None),
            P("tile", None),
            P(),
        ),
        out_specs=(P("year", "tile", None),) * 2,
        check_vma=False,
    )
```
